128 devices in a mesh: row: 16 (over z, y), col: 8 (over x, core).
Axes of the slice: x: 4, y: 4, z: 4, core: 2. Of those that a mesh axis runs over, the one named last changes fastest.
Arguments:
- panel_blocks: bfloat16 [8192, 2048], P('row', 'col'), may hold values from -4 to 4
- live_rows: int32 [8, 32], P('col', 'row'), may hold values from 0 to 2, as said below
- window_blocks: bfloat16 [2048, 2048], P(None, 'col'), as said below
- diag_inverse: bfloat16 [8, 256, 256], P('col'), as said below
- trailing: float32 [8192, 8192], P('row', 'col'), may hold values from -6 to 6
Outputs:
- panel_factor: bfloat16 [8192, 2048], P('row', 'col')
- window_factor: bfloat16 [2048, 2048], P(None, 'col')
- trailing_out: float32 [8192, 8192], P('row', 'col')
The draws below stay inside these ranges and needn't reach their ends.
Inputs may be any that keep to these rules, and one draw needn't show every extreme that they name: `live_rows`: for each panel and row index the 2 entries are distinct local block rows in ascending order followed by 2 for empty slots; each row index has at least one live slot per panel; in every panel some row index has all 2 slots live and some other row index has an empty slot. `diag_inverse`: each matrix is lower triangular with a positive diagonal. `window_blocks`: entries lie within plus or minus 24 / sqrt(256).
All inputs are finite; a program needn't handle non-finite values.
Results may differ from the reference program's by a relative error of at most 0.009.
Values may be sent and summed in bfloat16 or wider, within the bound.
A program may use at most 128 MiB of HBM per device.

```python
import jax
import jax.numpy as jnp
from jax import lax

BLK = 256
RB_DEV = 2
LIVE = 2
PANELS = 8
NB = 32
N_ROW = 16


def draw_live_rows(key, part):
    key_count, key_force, key_order, key_empty = jax.random.split(jax.random.fold_in(key, 11), 4)
    counts = jax.random.randint(key_count, (PANELS, N_ROW), 1, LIVE + 1)
    forced = jax.random.randint(key_force, (PANELS, 1), 0, N_ROW)
    emptied = (forced + 1 + jax.random.randint(key_empty, (PANELS, 1), 0, N_ROW - 1)) % N_ROW
    positions = jnp.arange(N_ROW)[None, :]
    counts = jnp.where(positions == emptied, LIVE - 1, counts)
    counts = jnp.where(positions == forced, LIVE, counts)
    scores = jax.random.randint(key_order, (PANELS, N_ROW, RB_DEV), 0, 1 << 20) * RB_DEV + jnp.arange(RB_DEV)[None, None, :]
    order = jnp.argsort(scores, axis=-1)[:, :, :LIVE]
    chosen = jnp.where(jnp.arange(LIVE)[None, None, :] < counts[:, :, None], order, RB_DEV)
    chosen = jnp.sort(chosen, axis=-1)
    return chosen.reshape(PANELS, N_ROW * LIVE).astype(jnp.int32)


def draw_window_blocks(key, part):
    key_window = jax.random.fold_in(key, 37)
    spread_scale = 9.6 / BLK ** 0.5
    entries = jnp.clip(jax.random.normal(key_window, (PANELS * BLK, PANELS * BLK), jnp.float32), -2.5, 2.5)
    return (entries * spread_scale).astype(jnp.bfloat16)


def draw_diag_inverse(key, part):
    key_diag, key_off = jax.random.split(jax.random.fold_in(key, 23))
    diagonal = jax.random.uniform(key_diag, (PANELS, BLK), jnp.float32, 0.07, 0.16)
    lower = jax.random.normal(key_off, (PANELS, BLK, BLK), jnp.float32) * 0.11 / BLK ** 0.5
    lower = jnp.tril(lower, -1) + jnp.eye(BLK, dtype=jnp.float32)[None] * diagonal[:, :, None]
    return lower.astype(jnp.bfloat16)


def steps_of(own_key, extent, cuts, low, high):
    loudness, own = 1.0, jax.random.fold_in(own_key, 6)
    for axis_at, shards_of in cuts:
        steps = jnp.exp(jax.random.uniform(jax.random.fold_in(own, axis_at), (shards_of,), jnp.float32, low / len(cuts), high / len(cuts)))
        loudness = loudness * jnp.repeat(steps, extent[axis_at] // shards_of).reshape([-1 if axis == axis_at else 1 for axis in range(len(extent))])
    return loudness


def bell_draw(own_key, shape, scale, limit, cuts=(), kind=jnp.bfloat16):
    drawn = jax.random.normal(own_key, shape, jnp.float32) * scale
    if len(cuts) > 0:
        drawn = steps_of(own_key, shape, cuts, -0.22, 0.18) * drawn
    return jnp.clip(drawn, min=-limit, max=limit).astype(kind)


def setup_inputs(seed: int = 0) -> dict:
    splits = jax.random.split(jax.random.key(seed), 6)
    panel_blocks = bell_draw(splits[0], (N_ROW * LIVE * BLK, PANELS * BLK), 1.0, 4.0, ((0, 16), (1, 8)))
    live_rows = draw_live_rows(jax.random.fold_in(splits[5], 71), 0)
    window_blocks = draw_window_blocks(jax.random.fold_in(splits[5], 71), 0)
    diag_inverse = draw_diag_inverse(jax.random.fold_in(splits[5], 71), 0)
    trailing = bell_draw(splits[4], (NB * BLK, NB * BLK), 1.0, 6.0, ((0, 16), (1, 8)), jnp.float32)
    return {"panel_blocks": panel_blocks, "live_rows": live_rows, "window_blocks": window_blocks, "diag_inverse": diag_inverse, "trailing": trailing}


def reference(panel_blocks, live_rows, window_blocks, diag_inverse, trailing):
    width = BLK
    slots = N_ROW * LIVE
    lanes = jnp.arange(PANELS * width) // width
    valid = live_rows < RB_DEV
    panel_out = []
    window_cols = []
    for p in range(PANELS):
        acc = panel_blocks[:, p * width:(p + 1) * width].astype(jnp.float32)
        accw = window_blocks[:, p * width:(p + 1) * width].astype(jnp.float32)
        here = live_rows[p].reshape(N_ROW, LIVE)
        for q in range(p):
            there = live_rows[q].reshape(N_ROW, LIVE)
            match = ((here[:, :, None] == there[:, None, :]) & (here[:, :, None] < RB_DEV)).astype(jnp.float32)
            picked = jnp.einsum('rst,rtab->rsab', match, panel_out[q].astype(jnp.float32).reshape(N_ROW, LIVE, width, width))
            picked = picked.reshape(slots * width, width).astype(jnp.bfloat16)
            w_pq = window_cols[q][p * width:(p + 1) * width]
            acc = acc - jnp.dot(picked, w_pq.T, preferred_element_type=jnp.float32)
            accw = accw - jnp.dot(window_cols[q], w_pq.T, preferred_element_type=jnp.float32)
        inverse = diag_inverse[p]
        keep = jnp.repeat(valid[p], width)[:, None]
        solved = jnp.dot(acc.astype(jnp.bfloat16), inverse.T, preferred_element_type=jnp.float32)
        panel_out.append(jnp.where(keep, solved, 0.0).astype(jnp.bfloat16))
        solved_w = jnp.dot(accw.astype(jnp.bfloat16), inverse.T, preferred_element_type=jnp.float32)
        window_cols.append(jnp.where((lanes > p)[:, None], solved_w, 0.0).astype(jnp.bfloat16))
    total_rows = RB_DEV * N_ROW
    spread_cols = []
    for p in range(PANELS):
        here = live_rows[p].reshape(N_ROW, LIVE)
        onehot = (here[:, :, None] == jnp.arange(RB_DEV)[None, None, :]).astype(jnp.float32)
        spread = jnp.einsum('rsi,rsab->riab', onehot, panel_out[p].astype(jnp.float32).reshape(N_ROW, LIVE, width, width))
        spread_cols.append(spread.reshape(total_rows * width, width))
    factor_all = jnp.concatenate(spread_cols, axis=1)
    trailing_out = trailing - jnp.dot(factor_all, factor_all.T, precision=lax.Precision.HIGHEST, preferred_element_type=jnp.float32)
    return jnp.concatenate(panel_out, axis=1), jnp.concatenate(window_cols, axis=1), trailing_out
```

```python
import functools

import jax
import jax.numpy as jnp
from jax import lax
from jax.experimental import pallas as pl
from jax.experimental.pallas import tpu as pltpu
from jax.sharding import PartitionSpec as P

B = 256
S = 16
N = 8
BF = jnp.bfloat16
F32 = jnp.float32
MESH = pl.DeviceIdType.MESH


def place():
    row = lax.axis_index("row")
    col = lax.axis_index("col")
    return row, col, col // 2, row % 4, row // 4, col % 2


def bits_of(y, z):
    return [((y + 1) // 2) % 2, ((z + 1) // 2) % 2, y // 2, z // 2]


def address(bits, k):
    return sum(bits[(k + i) % 4] * 2**i for i in range(4))


def partners(y, z):
    ya = y + 1 - 2 * (y % 2)
    za = z + 1 - 2 * (z % 2)
    return [z * 4 + ya, za * 4 + y, z * 4 + 3 - y, (3 - z) * 4 + y]


def gather_kernel(
    win, inv, pan, wg, arow, acol,
    wx_recv, wx_send, wh_recv, wh_send, wd_recv, wd_send,
    as_recv, as_send, ah_recv, ah_send, ar_recv, ar_send, lsem,
):
    row, col, x, y, z, core = place()
    bits = bits_of(y, z)
    addr = [address(bits, k) for k in range(4)]
    other = 1 - core

    def pick(a, b, c):
        return a * (1 - c) + b * c

    def remote(src, dst, ssem, rsem, r, c):
        return pltpu.make_async_remote_copy(
            src_ref=src, dst_ref=dst, send_sem=ssem, recv_sem=rsem, device_id=(r, c), device_id_type=MESH
        )

    def lanes(c):
        return pl.ds(pl.multiple_of(c * B, B), B)

    def rows(start, count):
        return pl.ds(pl.multiple_of(start, S), count)

    for j in range(4):

        @pl.when(x <= j)
        def _():
            for kc in range(2):
                q = 2 * j + kc
                t = addr[j] if kc == 0 else addr[3 - j]
                dst = wg.at[rows(q * B + t * S, S), lanes(col)]

                def send(src):
                    for d in range(4):
                        target = (x + d) % 4 * 2 + kc
                        if d == 0:

                            @pl.when(core == kc)
                            def _():
                                pltpu.make_async_copy(src, dst, wx_recv.at[j]).start()

                            @pl.when(core != kc)
                            def _():
                                remote(src, dst, wx_send.at[j], wx_recv.at[j], row, target).start()
                        else:
                            remote(src, dst, wx_send.at[j], wx_recv.at[j], row, target).start()

                @pl.when(q == col)
                def _():
                    send(inv.at[rows(t * S, S), :])

                @pl.when(q != col)
                def _():
                    send(win.at[rows(q * B + t * S, S), :])

    h = y % 2

    def scatter(t, carry):
        ty, tz = t % 4, t // 4
        tbits = bits_of(ty, tz)
        tcol = 2 * z + y // 2
        mine = (t == row) & (tcol == col)
        for kk in range(2):
            s = pick(address(tbits, kk), address(tbits, 2 + kk), h)
            src = pan.at[rows(kk * B + s * S, S), :]
            k = 2 * h + kk
            dst = acol.at[rows(k * B + s * S, S), lanes(col)]

            @pl.when(mine)
            def _():
                pltpu.make_async_copy(src, dst, as_recv.at[k]).start()

            @pl.when(jnp.logical_not(mine))
            def _():
                remote(src, dst, as_send, as_recv.at[k], t, tcol).start()

        return carry

    lax.fori_loop(0, 16, scatter, 0)

    dst = arow.at[:, lanes(col)]
    pltpu.make_async_copy(pan, dst, lsem).start()
    for d in range(1, 4):
        remote(pan, dst, ar_send.at[d - 1], ar_recv.at[col], row, (x + d) % 4 * 2 + core).start()
    remote(pan, dst, ar_send.at[3], ar_recv.at[col], row, x * 2 + other).start()

    near = partners(y, z)
    for i in range(4):
        n = 2**i
        for j in range(4):
            k_addr = pick(addr[j], addr[3 - j], core)
            q = 2 * j + core
            width = B * (2 * j + 2)
            if i == 0:
                got = wg.at[rows(q * B + k_addr * S, S), pl.ds(0, width)]
                pltpu.make_async_copy(got, got, wx_recv.at[j]).wait()
            else:
                m = n // 2
                base = k_addr // n * n + (1 - k_addr // m % 2) * m
                got = wg.at[rows(q * B + base * S, m * S), pl.ds(0, width)]
                pltpu.make_async_copy(got, got, wh_recv.at[i - 1, j]).wait()
            base = k_addr // n * n
            part = wg.at[rows(q * B + base * S, n * S), pl.ds(0, width)]
            to = pick(near[(j + i) % 4], near[(3 - j + i) % 4], core)
            remote(part, part, wh_send.at[i, j], wh_recv.at[i, j], to, col).start()
        for k in range(4):
            if i == 0:
                got = acol.at[rows(k * B + addr[k] * S, S), :]
                pltpu.make_async_copy(got, got, as_recv.at[k]).wait()
            else:
                m = n // 2
                base = addr[k] // n * n + (1 - addr[k] // m % 2) * m
                got = acol.at[rows(k * B + base * S, m * S), :]
                pltpu.make_async_copy(got, got, ah_recv.at[i - 1, k]).wait()
            base = addr[k] // n * n
            part = acol.at[rows(k * B + base * S, n * S), :]
            remote(part, part, ah_send.at[i, k], ah_recv.at[i, k], near[(k + i) % 4], col).start()

    for d in range(1, 4):
        c = (x + 4 - d) % 4 * 2 + core
        got = arow.at[:, lanes(c)]
        pltpu.make_async_copy(got, got, ar_recv.at[c]).wait()
        remote(got, got, ar_send.at[3 + d], ar_recv.at[c], row, x * 2 + other).start()
    for j in range(4):
        k_addr = pick(addr[j], addr[3 - j], core)
        q = 2 * j + core
        width = B * (2 * j + 2)
        base = (1 - k_addr // 8) * 8
        got = wg.at[rows(q * B + base * S, 8 * S), pl.ds(0, width)]
        pltpu.make_async_copy(got, got, wh_recv.at[3, j]).wait()
        part = wg.at[rows(q * B, B), pl.ds(0, width)]
        remote(part, part, wd_send.at[j], wd_recv.at[j], row, x * 2 + other).start()

    for k in range(4):
        base = (1 - addr[k] // 8) * 8
        got = acol.at[rows(k * B + base * S, 8 * S), :]
        pltpu.make_async_copy(got, got, ah_recv.at[3, k]).wait()
    for j in range(4):
        width = B * (2 * j + 2)
        got = wg.at[rows((2 * j + other) * B, B), pl.ds(0, width)]
        pltpu.make_async_copy(got, got, wd_recv.at[j]).wait()
        part = wg.at[rows((2 * j + core) * B, B), pl.ds(0, width)]
        pltpu.make_async_copy(part, part, wd_send.at[j]).wait()

        @pl.when(x <= j)
        def _():
            sent = pan.at[pl.ds(0, 7 * S), :]
            pltpu.make_async_copy(sent, sent, wx_send.at[j]).wait()

    for d in range(4):
        c = (x + d) % 4 * 2 + other
        got = arow.at[:, lanes(c)]
        pltpu.make_async_copy(got, got, ar_recv.at[c]).wait()
    pltpu.make_async_copy(pan, arow.at[:, lanes(col)], lsem).wait()
    for d in range(7):
        pltpu.make_async_copy(pan, pan, ar_send.at[d]).wait()
    own = (z == x) & (y // 2 == core)

    @pl.when(own)
    def _():
        sent = pan.at[pl.ds(0, 30 * S), :]
        pltpu.make_async_copy(sent, sent, as_send).wait()

    @pl.when(jnp.logical_not(own))
    def _():
        pltpu.make_async_copy(pan, pan, as_send).wait()

    for i in range(4):
        n = 2**i
        for j in range(4):
            k_addr = pick(addr[j], addr[3 - j], core)
            q = 2 * j + core
            width = B * (2 * j + 2)
            part = wg.at[rows(q * B + k_addr // n * n * S, n * S), pl.ds(0, width)]
            pltpu.make_async_copy(part, part, wh_send.at[i, j]).wait()
            part = acol.at[rows(j * B + addr[j] // n * n * S, n * S), :]
            pltpu.make_async_copy(part, part, ah_send.at[i, j]).wait()


def gather(win, inv, pan):
    dma = pltpu.SemaphoreType.DMA
    anys = pl.BlockSpec(memory_space=pl.ANY)
    return pl.pallas_call(
        gather_kernel,
        out_shape=(
            jax.ShapeDtypeStruct((N * B, N * B), BF),
            jax.ShapeDtypeStruct((2 * B, N * B), BF),
            jax.ShapeDtypeStruct((4 * B, N * B), BF),
        ),
        in_specs=[anys] * 3,
        out_specs=(anys,) * 3,
        scratch_shapes=[
            dma((4,)), dma((4,)), dma((4, 4)), dma((4, 4)), dma((4,)), dma((4,)),
            dma((4,)), dma(()), dma((4, 4)), dma((4, 4)), dma((8,)), dma((7,)), dma(()),
        ],
        compiler_params=pltpu.CompilerParams(has_side_effects=True),
        name="gather",
    )(win, inv, pan)


def nt(a, b):
    return lax.dot_general(a, b, (((1,), (1,)), ((), ())), preferred_element_type=F32)


def factor_kernel(live, at, wg, arow, acol, trail, pan_out, win_out, trail_out, wf, frow, fcol):
    row, col = at[0], at[1]

    def lane(p):
        return slice(p * B, p * B + B)

    for p in range(N):
        inv = wg[p * B : (p + 1) * B, lane(p)]
        prev = slice(0, p * B)

        def solve(raw, factors, ref_rows):
            acc = raw.astype(F32)
            if p > 0:
                acc = acc - nt(factors[ref_rows, prev], wf[p * B : (p + 1) * B, prev])
            return nt(acc.astype(BF), inv)

        def window_tile(q, carry):
            at_rows = pl.ds(pl.multiple_of(q * B, B), B)
            wf[at_rows, lane(p)] = solve(wg[at_rows, lane(p)], wf, at_rows).astype(BF)
            return carry

        lax.fori_loop(p + 1, N, window_tile, 0)

        def slots(src, dst, r, first):
            l0 = live[p, 2 * r]
            l1 = live[p, 2 * r + 1]
            for i in range(2):
                at_rows = slice(first + i * B, first + i * B + B)
                if i == 0:
                    raw = src[at_rows, lane(p)]
                    keep = l0 == 0
                else:
                    raw = jnp.where(l0 == 1, src[first : first + B, lane(p)], src[at_rows, lane(p)])
                    keep = (l0 == 1) | (l1 == 1)
                out = jnp.where(keep, solve(raw, dst, at_rows), 0.0)
                dst[at_rows, lane(p)] = out.astype(BF)

        slots(arow, frow, row, 0)
        for s in range(2):
            slots(acol, fcol, 2 * col + s, s * 2 * B)

    mine = pl.ds(pl.multiple_of(col * B, B), B)
    for q in range(N):
        block = wf[q * B : (q + 1) * B, mine]
        win_out[q * B : (q + 1) * B, :] = jnp.where(q > col, block, jnp.zeros_like(block))
    l0 = live[col, 2 * row]
    l1 = live[col, 2 * row + 1]
    f0 = frow[0:B, mine]
    f1 = frow[B : 2 * B, mine]
    pan_out[0:B, :] = jnp.where(l0 == 0, f0, f1)
    pan_out[B : 2 * B, :] = jnp.where(l1 == 1, f1, jnp.zeros_like(f1))
    for k in range(4):
        here = slice(k * B, k * B + B)
        trail_out[:, here] = trail[:, here] - nt(frow[...], fcol[here, :])


def factor(live, at, wg, arow, acol, trail):
    vmem = pl.BlockSpec(memory_space=pltpu.VMEM)
    smem = pl.BlockSpec(memory_space=pltpu.SMEM)
    return pl.pallas_call(
        factor_kernel,
        out_shape=(
            jax.ShapeDtypeStruct((2 * B, B), BF),
            jax.ShapeDtypeStruct((N * B, B), BF),
            jax.ShapeDtypeStruct(trail.shape, F32),
        ),
        in_specs=[smem, smem, vmem, vmem, vmem, vmem],
        out_specs=(vmem,) * 3,
        scratch_shapes=[
            pltpu.VMEM((N * B, N * B), BF),
            pltpu.VMEM((2 * B, N * B), BF),
            pltpu.VMEM((4 * B, N * B), BF),
        ],
        compiler_params=pltpu.CompilerParams(vmem_limit_bytes=56 * 2**20),
        name="factor",
    )(live, at, wg, arow, acol, trail)


def local(panel_blocks, live_rows, window_blocks, diag_inverse, trailing):
    live = lax.all_gather(live_rows, "row", axis=1, tiled=True)
    live = lax.all_gather(live, "col", axis=0, tiled=True)
    at = jnp.stack([lax.axis_index("row"), lax.axis_index("col")]).astype(jnp.int32)
    wg, arow, acol = gather(window_blocks, diag_inverse[0], panel_blocks)
    return factor(live, at, wg, arow, acol, trailing)


def solution(mesh):
    return jax.shard_map(
        local,
        mesh=mesh,
        in_specs=(
            P("row", "col"),
            P("col", "row"),
            P(None, "col"),
            P("col", None, None),
            P("row", "col"),
        ),
        out_specs=(P("row", "col"), P(None, "col"), P("row", "col")),
        check_vma=False,
    )
```

```python
import jax
import jax.numpy as jnp
from jax import lax
from jax.experimental import pallas as pl
from jax.experimental.pallas import tpu as pltpu
from jax.sharding import PartitionSpec as P

B = 256
S = 16
H = 128
N = 8
BF = jnp.bfloat16
F32 = jnp.float32
MESH = pl.DeviceIdType.MESH


def place():
    row = lax.axis_index("row")
    col = lax.axis_index("col")
    return row, col, col // 2, row % 4, row // 4, col % 2


def bits_of(y, z):
    return [((y + 1) // 2) % 2, ((z + 1) // 2) % 2, y // 2, z // 2]


def address(bits, k):
    return sum(bits[(k + i) % 4] * 2**i for i in range(4))


def partners(y, z):
    ya = y + 1 - 2 * (y % 2)
    za = z + 1 - 2 * (z % 2)
    return [z * 4 + ya, za * 4 + y, z * 4 + 3 - y, (3 - z) * 4 + y]


def pick(a, b, c):
    return a * (1 - c) + b * c


def lanes(c):
    return pl.ds(pl.multiple_of(c * B, B), B)


def rows(start, count):
    return pl.ds(pl.multiple_of(start, S), count)


def lane(p):
    return slice(p * B, p * B + B)


def nt(a, b):
    return lax.dot_general(a, b, (((1,), (1,)), ((), ())), preferred_element_type=F32)


def kernel(
    live, win, inv, pan, trail, pan_out, win_out, trail_out,
    pv, kp, krow, kcol, wg, wf, u, ar, fr, am, fm, ao, tr, wo, po,
    wx_recv, wx_send, wh_recv, wh_send, wd_recv, wd_send,
    as_recv, as_send, ah_recv, ah_send, a3_recv, a3_send,
    ar_recv, ar_send, kr_recv, kr_send, kc_recv, kc_send, lsem, osem,
):
    row, col, x, y, z, core = place()
    bits = bits_of(y, z)
    addr = [address(bits, k) for k in range(4)]
    near = partners(y, z)
    other = 1 - core
    h = y % 2
    tcol = 2 * z + y // 2
    own = (z == x) & (y // 2 == core)

    def local(src, dst, sem):
        return pltpu.make_async_copy(src, dst, sem)

    def take(ref, sem):
        pltpu.make_async_copy(ref, ref, sem).wait()

    def remote(src, dst, ssem, rsem, r, c):
        return pltpu.make_async_remote_copy(
            src_ref=src, dst_ref=dst, send_sem=ssem, recv_sem=rsem, device_id=(r, c), device_id_type=MESH
        )

    load = local(pan, pv, lsem.at[0])
    load.start()
    load_trail = local(trail, tr, lsem.at[1])
    load_trail.start()

    barrier = pltpu.get_barrier_semaphore()

    def greet(r, c):
        pl.semaphore_signal(barrier, inc=1, device_id=(r, c), device_id_type=MESH)

    for d in range(1, 8):
        greet(row, (col + d) % 8)
    for k in range(4):
        greet(near[k], col)

    def greet_sources(t, carry):
        r, c = 2 * col + t // 8, t % 8

        @pl.when(jnp.logical_not((r == row) & (c == col)))
        def _():
            greet(r, c)

        return carry

    lax.fori_loop(0, 16, greet_sources, 0)

    l0 = live[0, 0]
    l1 = live[0, 1]
    load.wait()
    pv[B : 2 * B, :] = jnp.where(l0 == 1, pv[0:B, :], pv[B : 2 * B, :])
    keep0 = jnp.where(l0 == 0, 1.0, 0.0)
    keep1 = jnp.where((l0 == 1) | (l1 == 1), 1.0, 0.0)
    kp[...] = jnp.where(lax.broadcasted_iota(jnp.int32, (S, H), 0) == 0, keep0, keep1).astype(BF)

    pl.semaphore_wait(barrier, 27 - own.astype(jnp.int32))

    for j in range(4):

        @pl.when(x <= j)
        def _():
            for kc in range(2):
                q = 2 * j + kc
                t = addr[j] if kc == 0 else addr[3 - j]
                dst = wg.at[rows(q * B + t * S, S), lanes(col)]

                def send(src):
                    for d in range(4):
                        target = (x + d) % 4 * 2 + kc
                        if d == 0:

                            @pl.when(core == kc)
                            def _():
                                local(src, dst, wx_recv.at[j]).start()

                            @pl.when(core != kc)
                            def _():
                                remote(src, dst, wx_send.at[j], wx_recv.at[j], row, target).start()
                        else:
                            remote(src, dst, wx_send.at[j], wx_recv.at[j], row, target).start()

                @pl.when(q == col)
                def _():
                    send(inv.at[rows(t * S, S), :])

                @pl.when(q != col)
                def _():
                    send(win.at[rows(q * B + t * S, S), :])

    def scatter(t, carry):
        tbits = bits_of(t % 4, t // 4)
        mine = own & (t == row)
        kept = kcol.at[rows(h * S, S), pl.ds(pl.multiple_of(col * H, H), H)]

        @pl.when(mine)
        def _():
            local(kp, kept, kc_recv.at[h]).start()

        @pl.when(jnp.logical_not(mine))
        def _():
            remote(kp, kept, kc_send, kc_recv.at[h], t, tcol).start()

        for kk in range(2):
            s = pick(address(tbits, kk), address(tbits, 2 + kk), h)
            src = pv.at[rows(kk * B + s * S, S), :]
            k = 2 * h + kk
            dst = am.at[rows(k * H + s % 8 * S, S), lanes(col)]

            @pl.when(mine)
            def _():
                local(src, dst, as_recv.at[k]).start()

            @pl.when(jnp.logical_not(mine))
            def _():
                remote(src, dst, as_send, as_recv.at[k], t, tcol).start()

        return carry

    def w_base(j, i):
        n = 2**i
        return pick(addr[j], addr[3 - j], core) // n * n

    def w_part(j, base, n, c):
        return wg.at[rows((2 * j + c) * B + base * S, n * S), pl.ds(0, B * (2 * j + 2))]

    def w_got(j, i):
        n = 2**i
        a = pick(addr[j], addr[3 - j], core)
        return w_part(j, a // (2 * n) * (2 * n) + (1 - a // n % 2) * n, n, core)

    def w_step(i):
        for j in range(4):
            if i == 0:
                take(w_part(j, w_base(j, 0), 1, core), wx_recv.at[j])
            else:
                take(w_got(j, i - 1), wh_recv.at[i - 1, j])
            part = w_part(j, w_base(j, i), 2**i, core)
            to = pick(near[(j + i) % 4], near[(3 - j + i) % 4], core)
            remote(part, part, wh_send.at[i, j], wh_recv.at[i, j], to, col).start()
            if i == 3:
                remote(part, part, wd_send.at[j, 0], wd_recv.at[j, 0], row, x * 2 + other).start()

    def a_part(k, base, n):
        return am.at[rows(k * H + base * S, n * S), :]

    def a_got(k, i):
        n = 2**i
        a = addr[k] % 8
        return a_part(k, a // (2 * n) * (2 * n) + (1 - a // n % 2) * n, n)

    def a_step(i):
        n = 2**i
        for k in range(4):
            if i == 0:
                take(a_part(k, addr[k] % 8, 1), as_recv.at[k])
            else:
                take(a_got(k, i - 1), ah_recv.at[i - 1, k])
            if i < 3:
                part = a_part(k, addr[k] % 8 // n * n, n)
                remote(part, part, ah_send.at[i, k], ah_recv.at[i, k], near[(k + i) % 4], col).start()
        if i == 3:
            for g in range(4):
                for k in range(4):
                    there = slice(k * H, k * H + H), slice(g * 2 * B, g * 2 * B + 2 * B)
                    remote(
                        am.at[there], ao.at[there], a3_send.at[g, k], a3_recv.at[g, k], near[(k + 3) % 4], col
                    ).start()

    lax.fori_loop(0, 16, scatter, 0)
    w_step(0)

    mine = ar.at[:, lanes(col)]
    kept = krow.at[:, pl.ds(pl.multiple_of(col * H, H), H)]
    local(pv, mine, lsem.at[2]).start()
    local(kp, kept, kr_recv).start()
    for d in range(1, 8):
        remote(kp, kept, kr_send, kr_recv, row, (col + d) % 8).start()
    for d in range(1, 4):
        remote(pv, mine, ar_send.at[d - 1], ar_recv.at[col], row, (x + d) % 4 * 2 + core).start()
    remote(pv, mine, ar_send.at[3], ar_recv.at[col], row, x * 2 + other).start()

    w_step(1)
    a_step(0)
    w_step(2)
    a_step(1)
    w_step(3)
    a_step(2)

    for d in range(1, 4):
        c = (x + 4 - d) % 4 * 2 + core
        got = ar.at[:, lanes(c)]
        take(got, ar_recv.at[c])
        remote(got, got, ar_send.at[3 + d], ar_recv.at[c], row, x * 2 + other).start()
    for j in range(4):
        got = w_got(j, 3)
        take(got, wh_recv.at[3, j])
        remote(got, got, wd_send.at[j, 1], wd_recv.at[j, 1], row, x * 2 + other).start()
    a_step(3)
    for d in range(4):
        c = (x + d) % 4 * 2 + other
        take(ar.at[:, lanes(c)], ar_recv.at[c])
    local(pv, mine, lsem.at[2]).wait()
    take(krow, kr_recv)
    for j in range(4):
        a = pick(addr[3 - j], addr[j], core) // 8
        take(w_part(j, a * 8, 8, other), wd_recv.at[j, 0])
        take(w_part(j, (1 - a) * 8, 8, other), wd_recv.at[j, 1])

    def keep(ref, first, i, p):
        t = ref[first : first + S, p * H : p * H + H].astype(F32)[i : i + 1, :]
        return jnp.concatenate([t, t], axis=1) > 0.5

    def masked(value, mask):
        return jnp.where(mask, value, 0.0).astype(BF)

    for p in range(N):
        diag = wg[lane(p), lane(p)]
        if p > 0:
            prev = jnp.dot(diag, wf[lane(p), : p * B], preferred_element_type=F32)
            u[lane(p), : p * B] = (-prev).astype(BF)
        u[lane(p), lane(p)] = diag
        up = u[lane(p), : (p + 1) * B]

        def operand(factors, raw, at):
            if p == 0:
                return raw[at, lane(p)]
            return jnp.concatenate([factors[at, : p * B], raw[at, lane(p)]], axis=1)

        for q in range(p + 1, N):
            wf[lane(q), lane(p)] = nt(operand(wf, wg, lane(q)), up).astype(BF)
        for i in range(2):
            fr[lane(i), lane(p)] = masked(nt(operand(fr, ar, lane(i)), up), keep(krow, 0, i, p))

    here = lanes(col)
    for q in range(N):
        block = wf[lane(q), here]
        wo[lane(q), :] = jnp.where(q > col, block, jnp.zeros_like(block))
    local(wo, win_out, osem.at[0]).start()
    f0 = fr[0:B, here]
    f1 = fr[B : 2 * B, here]
    po[0:B, :] = jnp.where(l0 == 0, f0, f1)
    po[B : 2 * B, :] = jnp.where(l0 == 0, f1, jnp.zeros_like(f1))
    local(po, pan_out, osem.at[1]).start()

    take(kcol.at[0:S, :], kc_recv.at[0])
    take(kcol.at[S : 2 * S, :], kc_recv.at[1])

    def solve(p, factors, raw):
        up = u[lane(p), : (p + 1) * B]
        z_in = raw[:, lane(p)]
        if p > 0:
            z_in = jnp.concatenate([factors[:, : p * B], z_in], axis=1)
        out = nt(z_in, up)
        for k in range(4):
            part = slice(k * H, k * H + H)
            factors[part, lane(p)] = masked(out[part, :], keep(kcol, k // 2 * S, k % 2, p))

    load_trail.wait()

    def update(factors, far):
        for g in range(2):
            prod = nt(fr[...], factors[lane(g), :])
            for e in range(2):
                k = 2 * g + e
                half = addr[k] // 8
                if far:
                    half = 1 - half
                at = pl.ds(pl.multiple_of(k * B + half * H, H), H)
                tr[:, at] = tr[:, at] - prod[:, e * H : e * H + H]
                local(tr.at[:, at], trail_out.at[:, at], osem.at[2 + 4 * far + k]).start()

    for p in range(N):
        solve(p, fm, am)
    update(fm, 0)
    for p in range(N):
        if p % 2 == 0:
            for k in range(4):
                g = p // 2
                take(ao.at[k * H : k * H + H, g * 2 * B : g * 2 * B + 2 * B], a3_recv.at[g, k])
        solve(p, ao, ao)
    update(ao, 1)

    for j in range(4):

        @pl.when(x <= j)
        def _():
            take(pv.at[pl.ds(0, 7 * S), :], wx_send.at[j])

        for i in range(4):
            take(w_part(j, w_base(j, i), 2**i, core), wh_send.at[i, j])
        take(w_part(j, w_base(j, 3), 8, core), wd_send.at[j, 0])
        take(w_got(j, 3), wd_send.at[j, 1])
        for i in range(3):
            n = 2**i
            take(a_part(j, addr[j] % 8 // n * n, n), ah_send.at[i, j])
        for g in range(4):
            take(am.at[j * H : j * H + H, g * 2 * B : g * 2 * B + 2 * B], a3_send.at[g, j])
    for d in range(7):
        take(pv, ar_send.at[d])
    take(krow.at[:, 0 : 7 * H], kr_send)

    @pl.when(own)
    def _():
        take(pv.at[pl.ds(0, 30 * S), :], as_send)
        take(am.at[0:S, 0 : 15 * H], kc_send)

    @pl.when(jnp.logical_not(own))
    def _():
        take(pv, as_send)
        take(am.at[0:S, 0 : 16 * H], kc_send)

    local(wo, win_out, osem.at[0]).wait()
    local(po, pan_out, osem.at[1]).wait()
    for far in range(2):
        for k in range(4):
            half = addr[k] // 8
            if far:
                half = 1 - half
            at = pl.ds(pl.multiple_of(k * B + half * H, H), H)
            local(tr.at[:, at], trail_out.at[:, at], osem.at[2 + 4 * far + k]).wait()


def fused(live, win, inv, pan, trail):
    dma = pltpu.SemaphoreType.DMA
    anys = pl.BlockSpec(memory_space=pl.ANY)
    smem = pl.BlockSpec(memory_space=pltpu.SMEM)
    vmem = pltpu.VMEM
    return pl.pallas_call(
        kernel,
        out_shape=(
            jax.ShapeDtypeStruct((2 * B, B), BF),
            jax.ShapeDtypeStruct((N * B, B), BF),
            jax.ShapeDtypeStruct((2 * B, 4 * B), F32),
        ),
        in_specs=[smem] + [anys] * 4,
        out_specs=(anys,) * 3,
        scratch_shapes=[
            vmem((2 * B, B), BF),
            vmem((S, H), BF),
            vmem((S, N * H), BF),
            vmem((2 * S, N * H), BF),
            vmem((N * B, N * B), BF),
            vmem((N * B, N * B), BF),
            vmem((N * B, N * B), BF),
            vmem((2 * B, N * B), BF),
            vmem((2 * B, N * B), BF),
            vmem((2 * B, N * B), BF),
            vmem((2 * B, N * B), BF),
            vmem((2 * B, N * B), BF),
            vmem((2 * B, 4 * B), F32),
            vmem((N * B, B), BF),
            vmem((2 * B, B), BF),
            dma((4,)), dma((4,)), dma((4, 4)), dma((4, 4)), dma((4, 2)), dma((4, 2)),
            dma((4,)), dma(()), dma((3, 4)), dma((3, 4)), dma((4, 4)), dma((4, 4)),
            dma((8,)), dma((7,)), dma(()), dma(()), dma((2,)), dma(()), dma((3,)), dma((10,)),
        ],
        compiler_params=pltpu.CompilerParams(
            has_side_effects=True, collective_id=0, vmem_limit_bytes=58 * 2**20
        ),
        name="fused",
    )(live, win, inv, pan, trail)


def local_part(panel_blocks, live_rows, window_blocks, diag_inverse, trailing):
    return fused(live_rows, window_blocks, diag_inverse[0], panel_blocks, trailing)


def solution(mesh):
    return jax.shard_map(
        local_part,
        mesh=mesh,
        in_specs=(
            P("row", "col"),
            P("col", "row"),
            P(None, "col"),
            P("col", None, None),
            P("row", "col"),
        ),
        out_specs=(P("row", "col"), P(None, "col"), P("row", "col")),
        check_vma=False,
    )
```

```python
import jax
import jax.numpy as jnp
from jax import lax
from jax.experimental import pallas as pl
from jax.experimental.pallas import tpu as pltpu
from jax.sharding import PartitionSpec as P

B = 256
S = 16
H = 128
N = 8
BF = jnp.bfloat16
F32 = jnp.float32
MESH = pl.DeviceIdType.MESH


def place():
    row = lax.axis_index("row")
    col = lax.axis_index("col")
    return row, col, col // 2, row % 4, row // 4, col % 2


def bits_of(y, z):
    return [((y + 1) // 2) % 2, ((z + 1) // 2) % 2, y // 2, z // 2]


def address(bits, k):
    return sum(bits[(k + i) % 4] * 2**i for i in range(4))


def partners(y, z):
    ya = y + 1 - 2 * (y % 2)
    za = z + 1 - 2 * (z % 2)
    return [z * 4 + ya, za * 4 + y, z * 4 + 3 - y, (3 - z) * 4 + y]


def pick(a, b, c):
    return a * (1 - c) + b * c


def lanes(c):
    return pl.ds(pl.multiple_of(c * B, B), B)


def rows(start, count):
    return pl.ds(pl.multiple_of(start, S), count)


def lane(p):
    return slice(p * B, p * B + B)


def nt(a, b):
    return lax.dot_general(a, b, (((1,), (1,)), ((), ())), preferred_element_type=F32)


def kernel(
    live, win, inv, pan, trail, pan_out, win_out, trail_out,
    pv, pp, st, a0, kp, krow, kcol, iv, wc, wg, wf, u, ar, fr, am, fm, ao, tr, wo, po,
    wx_recv, wx_send, wh_recv, wh_send, wd_recv, wd_send, wr_recv, wr_send, we_recv, we_send,
    a1_recv, a1_send, a2_recv, a2_send, ah_recv, ah_send, a3_recv, a3_send,
    ar_recv, ar_send, ad_recv, ad_send, kr_recv, kr_send, kc_recv, kc_send, lsem, osem,
):
    row, col, x, y, z, core = place()
    bits = bits_of(y, z)
    addr = [address(bits, k) for k in range(4)]
    near = partners(y, z)
    other = 1 - core
    h = y % 2
    sibling = x * 2 + other
    own = (z == x) & (y // 2 == core)

    def local(src, dst, sem):
        return pltpu.make_async_copy(src, dst, sem)

    def take(ref, sem):
        pltpu.make_async_copy(ref, ref, sem).wait()

    def remote(src, dst, ssem, rsem, r, c):
        return pltpu.make_async_remote_copy(
            src_ref=src, dst_ref=dst, send_sem=ssem, recv_sem=rsem, device_id=(r, c), device_id_type=MESH
        )

    load = local(pan, pv, lsem.at[0])
    load.start()
    load_window = local(win, wc, lsem.at[1])
    load_window.start()
    load_inverse = local(inv, iv, lsem.at[3])
    load_inverse.start()
    load_trail = local(trail, tr, lsem.at[2])
    load_trail.start()

    barrier = pltpu.get_barrier_semaphore()

    def greet(r, c):
        pl.semaphore_signal(barrier, inc=1, device_id=(r, c), device_id_type=MESH)

    for d in range(1, 8):
        greet(row, (col + d) % 8)
    for d in range(1, 16):
        greet((row + d) % 16, col)

    l0 = live[0, 0]
    l1 = live[0, 1]
    load.wait()
    pv[B : 2 * B, :] = jnp.where(l0 == 1, pv[0:B, :], pv[B : 2 * B, :])
    keep0 = jnp.where(l0 == 0, 1.0, 0.0)
    keep1 = jnp.where((l0 == 1) | (l1 == 1), 1.0, 0.0)
    kp[...] = jnp.where(lax.broadcasted_iota(jnp.int32, (S, H), 0) == 0, keep0, keep1).astype(BF)
    for t in range(16):
        tbits = bits_of(t % 4, t // 4)
        for kk in range(2):
            s = pick(address(tbits, kk), address(tbits, 2 + kk), h)
            pp[t * 2 * S + kk * S : t * 2 * S + kk * S + S, :] = pv[rows(kk * B + s * S, S), :]

    pl.semaphore_wait(barrier, 22)

    mine = st.at[rows(row * 2 * S, 2 * S), :]
    local(pp.at[rows(row * 2 * S, 2 * S), :], mine, a1_recv).start()

    def scatter(d, carry):
        t = (row + d) % 16
        remote(pp.at[rows(t * 2 * S, 2 * S), :], mine, a1_send, a1_recv, t, col).start()
        return carry

    lax.fori_loop(1, 16, scatter, 0)

    load_window.wait()
    load_inverse.wait()
    wc[lanes(col), :] = iv[...]
    for j in range(4):

        @pl.when(x <= (0, 1, 0, 2)[j])
        def _():
            for kc in range(2):
                t = addr[j] if kc == 0 else addr[3 - j]
                at = rows((2 * j + kc) * B + t * S, S)
                src = wc.at[at, :]
                dst = wg.at[at, lanes(col)]
                for d in range(4):
                    target = (x + d) % 4 * 2 + kc
                    if d == 0:

                        @pl.when(core == kc)
                        def _():
                            local(src, dst, wx_recv.at[j]).start()

                        @pl.when(core != kc)
                        def _():
                            remote(src, dst, wx_send.at[j], wx_recv.at[j], row, target).start()
                    else:
                        remote(src, dst, wx_send.at[j], wx_recv.at[j], row, target).start()

    def w_width(j):
        return (2, 4, 2, 6)[j] * B

    def w_base(j, i):
        n = 2**i
        return pick(addr[j], addr[3 - j], core) // n * n

    def w_part(j, base, n, c):
        return wg.at[rows((2 * j + c) * B + base * S, n * S), pl.ds(0, w_width(j))]

    def w_got(j, i):
        n = 2**i
        a = pick(addr[j], addr[3 - j], core)
        return w_part(j, a // (2 * n) * (2 * n) + (1 - a // n % 2) * n, n, core)

    def w_step(i):
        for j in range(4):
            if i == 0:
                take(w_part(j, w_base(j, 0), 1, core), wx_recv.at[j])
            else:
                take(w_got(j, i - 1), wh_recv.at[i - 1, j])
            part = w_part(j, w_base(j, i), 2**i, core)
            to = pick(near[(j + i) % 4], near[(3 - j + i) % 4], core)
            remote(part, part, wh_send.at[i, j], wh_recv.at[i, j], to, col).start()
            if i == 3:
                remote(part, part, wd_send.at[j, 0], wd_recv.at[j, 0], row, sibling).start()

    def a_part(k, base, n, g):
        return am.at[rows(k * H + base * S, n * S), slice(g * 4 * B, g * 4 * B + 4 * B)]

    def a_got(k, i, g):
        n = 2**i
        a = addr[k] % 8
        return a_part(k, a // (2 * n) * (2 * n) + (1 - a // n % 2) * n, n, g)

    def a_step(i, g):
        n = 2**i
        chunk = slice(g * 4 * B, g * 4 * B + 4 * B)
        if i == 0:
            take(a0.at[:, chunk], a2_recv.at[g])
            for k in range(4):
                am[rows(k * H + addr[k] % 8 * S, S), chunk] = a0[k * S : k * S + S, chunk]
        for k in range(4):
            if i > 0:
                take(a_got(k, i - 1, g), ah_recv.at[i - 1, g, k])
            if i < 3:
                part = a_part(k, addr[k] % 8 // n * n, n, g)
                remote(part, part, ah_send.at[i, g, k], ah_recv.at[i, g, k], near[(k + i) % 4], col).start()
        if i == 3:
            for g2 in (2 * g, 2 * g + 1):
                for k in range(4):
                    there = slice(k * H, k * H + H), slice(g2 * 2 * B, g2 * 2 * B + 2 * B)
                    remote(
                        am.at[there], ao.at[there], a3_send.at[g2, k], a3_recv.at[g2, k], near[(k + 3) % 4], col
                    ).start()

    pieces = [(1, 0), (2, 0), (3, 1)]

    def piece(n, c):
        xs, hf = pieces[n]
        return (4 + 2 * hf) * B, lanes(2 * xs + c)

    def whole_send(n):
        xs, hf = pieces[n]

        @pl.when(x == xs)
        def _():
            first, at = piece(n, core)
            src = wc.at[first : first + 2 * B, :]
            dst = wg.at[first : first + 2 * B, at]
            local(src, dst, wr_recv.at[n]).start()
            for d in range(1, 4):
                remote(src, dst, wr_send.at[n, d - 1], wr_recv.at[n], row, (x + d) % 4 * 2 + core).start()

    def whole_share(n):
        xs, hf = pieces[n]
        first, at = piece(n, core)
        got = wg.at[first : first + 2 * B, at]
        take(got, wr_recv.at[n])
        remote(got, got, we_send.at[n], we_recv.at[n], row, sibling).start()

    def whole_take(n):
        first, at = piece(n, other)
        take(wg.at[first : first + 2 * B, at], we_recv.at[n])

    w_step(0)
    take(st, a1_recv)
    for d in range(4):
        xd = (x + d) % 4
        for kc in range(2):
            src = st.at[rows((4 * xd + 2 * kc) * 2 * S, 4 * S), :]
            dst = a0.at[:, lanes(col)]
            if d == 0:

                @pl.when(core == kc)
                def _():
                    local(src, dst, a2_recv.at[x // 2]).start()

                @pl.when(core != kc)
                def _():
                    remote(src, dst, a2_send, a2_recv.at[x // 2], row, sibling).start()
            else:
                remote(src, dst, a2_send, a2_recv.at[x // 2], row, xd * 2 + kc).start()

    w_step(1)
    kept = krow.at[:, pl.ds(pl.multiple_of(col * H, H), H)]
    local(kp, kept, kr_recv).start()
    for d in range(1, 8):
        remote(kp, kept, kr_send, kr_recv, row, (col + d) % 8).start()
    for n in range(len(pieces)):
        whole_send(n)
    w_step(2)
    a_step(0, 0)
    a_step(0, 1)
    w_step(3)

    panel = ar.at[:, lanes(col)]
    local(pv, panel, lsem.at[0]).start()
    for d in range(1, 4):
        remote(pv, panel, ar_send.at[d - 1], ar_recv.at[d - 1], row, (x + d) % 4 * 2 + core).start()
    remote(pv, panel, ad_send.at[0], ad_recv.at[0], row, sibling).start()

    a_step(1, 0)
    a_step(1, 1)

    take(krow, kr_recv)

    @pl.when(own)
    def _():
        dst = kcol.at[rows(h * S, S), :]
        local(krow, dst, kc_recv.at[h]).start()
        for d in range(1, 16):
            remote(krow, dst, kc_send, kc_recv.at[h], (row + d) % 16, col).start()

    for j in range(4):
        got = w_got(j, 3)
        take(got, wh_recv.at[3, j])
        remote(got, got, wd_send.at[j, 1], wd_recv.at[j, 1], row, sibling).start()
    a_step(2, 0)
    a_step(2, 1)
    for n in range(len(pieces)):
        whole_share(n)
    for j in range(4):
        a = pick(addr[3 - j], addr[j], core) // 8
        take(w_part(j, a * 8, 8, other), wd_recv.at[j, 0])
        take(w_part(j, (1 - a) * 8, 8, other), wd_recv.at[j, 1])

    def keep(ref, first, i, p):
        t = ref[first : first + S, p * H : p * H + H].astype(F32)[i : i + 1, :]
        return jnp.concatenate([t, t], axis=1) > 0.5

    def masked(value, mask):
        return jnp.where(mask, value, 0.0).astype(BF)

    def operand(factors, raw, at, p):
        if p == 0:
            return raw[at, lane(p)]
        return jnp.concatenate([factors[at, : p * B], raw[at, lane(p)]], axis=1)

    for p in range(N):
        if p == 2:
            whole_take(0)
        if p == 4:
            a_step(3, 0)
        if p == 6:
            a_step(3, 1)
        if p == 4:
            whole_take(1)
        if p == 6:
            whole_take(2)
        diag = wg[lane(p), lane(p)]
        if p > 0:
            prev = jnp.dot(diag, wf[lane(p), : p * B], preferred_element_type=F32)
            u[lane(p), : p * B] = (-prev).astype(BF)
        u[lane(p), lane(p)] = diag
        up = u[lane(p), : (p + 1) * B]
        for q in range(p + 1, N):
            wf[lane(q), lane(p)] = nt(operand(wf, wg, lane(q), p), up).astype(BF)

    here = lanes(col)
    for q in range(N):
        block = wf[lane(q), here]
        wo[lane(q), :] = jnp.where(q > col, block, jnp.zeros_like(block))
    local(wo, win_out, osem.at[0]).start()

    take(kcol.at[0:S, :], kc_recv.at[0])
    take(kcol.at[S : 2 * S, :], kc_recv.at[1])

    def solve(p, factors, raw):
        up = u[lane(p), : (p + 1) * B]
        out = nt(operand(factors, raw, slice(0, 2 * B), p), up)
        for k in range(4):
            part = slice(k * H, k * H + H)
            factors[part, lane(p)] = masked(out[part, :], keep(kcol, k // 2 * S, k % 2, p))

    def update(factors, far, first, last):
        for g in range(2):
            prod = nt(fr[:, first:last], factors[lane(g), first:last])
            for e in range(2):
                k = 2 * g + e
                half = addr[k] // 8
                if far:
                    half = 1 - half
                at = pl.ds(pl.multiple_of(k * B + half * H, H), H)
                tr[:, at] = tr[:, at] - prod[:, e * H : e * H + H]
                if last == N * B:
                    local(tr.at[:, at], trail_out.at[:, at], osem.at[2 + 4 * far + k]).start()

    def solve_far(p):
        if p % 2 == 0:
            for k in range(4):
                g = p // 2
                take(ao.at[k * H : k * H + H, g * 2 * B : g * 2 * B + 2 * B], a3_recv.at[g, k])
        solve(p, ao, ao)

    for d in range(1, 4):
        got = ar.at[:, lanes((x + 4 - d) % 4 * 2 + core)]
        take(got, ar_recv.at[d - 1])
        remote(got, got, ad_send.at[d], ad_recv.at[d], row, sibling).start()
    local(pv, panel, lsem.at[0]).wait()
    for d in range(4):
        take(ar.at[:, lanes((x + 4 - d) % 4 * 2 + other)], ad_recv.at[d])
    for p in range(N):
        solve(p, fm, am)
    for p in range(N):
        up = u[lane(p), : (p + 1) * B]
        for i in range(2):
            fr[lane(i), lane(p)] = masked(nt(operand(fr, ar, lane(i), p), up), keep(krow, 0, i, p))
    f0 = fr[0:B, here]
    f1 = fr[B : 2 * B, here]
    po[0:B, :] = jnp.where(l0 == 0, f0, f1)
    po[B : 2 * B, :] = jnp.where(l0 == 0, f1, jnp.zeros_like(f1))
    local(po, pan_out, osem.at[1]).start()

    load_trail.wait()
    update(fm, 0, 0, N * B)
    for p in range(4):
        solve_far(p)

    solve_far(4)
    solve_far(5)
    update(ao, 1, 0, 6 * B)
    solve_far(6)
    solve_far(7)
    update(ao, 1, 6 * B, N * B)

    for j in range(4):

        @pl.when(x <= (0, 1, 0, 2)[j])
        def _():
            take(pv.at[pl.ds(0, 7 * S), :], wx_send.at[j])

        for i in range(4):
            take(w_part(j, w_base(j, i), 2**i, core), wh_send.at[i, j])
        take(w_part(j, w_base(j, 3), 8, core), wd_send.at[j, 0])
        take(w_got(j, 3), wd_send.at[j, 1])
        for i in range(3):
            n = 2**i
            for g in range(2):
                take(a_part(j, addr[j] % 8 // n * n, n, g), ah_send.at[i, g, j])
        for g in range(4):
            take(am.at[j * H : j * H + H, g * 2 * B : g * 2 * B + 2 * B], a3_send.at[g, j])
    take(pv.at[pl.ds(0, 15 * 2 * S), :], a1_send)
    take(pv.at[pl.ds(0, 7 * 4 * S), :], a2_send)
    for n in range(len(pieces)):
        xs, hf = pieces[n]
        take(pv, we_send.at[n])

        @pl.when(x == xs)
        def _():
            for d in range(3):
                take(pv, wr_send.at[n, d])

    for d in range(4):
        take(pv, ad_send.at[d])
        if d < 3:
            take(pv, ar_send.at[d])
    take(krow.at[:, 0 : 7 * H], kr_send)

    @pl.when(own)
    def _():
        take(ar.at[0 : 15 * S, 0 : N * H], kc_send)

    local(wo, win_out, osem.at[0]).wait()
    local(po, pan_out, osem.at[1]).wait()
    for far in range(2):
        for k in range(4):
            half = addr[k] // 8
            if far:
                half = 1 - half
            at = pl.ds(pl.multiple_of(k * B + half * H, H), H)
            local(tr.at[:, at], trail_out.at[:, at], osem.at[2 + 4 * far + k]).wait()


def fused(live, win, inv, pan, trail):
    dma = pltpu.SemaphoreType.DMA
    anys = pl.BlockSpec(memory_space=pl.ANY)
    smem = pl.BlockSpec(memory_space=pltpu.SMEM)
    vmem = pltpu.VMEM
    return pl.pallas_call(
        kernel,
        out_shape=(
            jax.ShapeDtypeStruct((2 * B, B), BF),
            jax.ShapeDtypeStruct((N * B, B), BF),
            jax.ShapeDtypeStruct((2 * B, 4 * B), F32),
        ),
        in_specs=[smem] + [anys] * 4,
        out_specs=(anys,) * 3,
        scratch_shapes=[
            vmem((2 * B, B), BF),
            vmem((2 * B, B), BF),
            vmem((2 * B, B), BF),
            vmem((4 * S, N * B), BF),
            vmem((S, H), BF),
            vmem((S, N * H), BF),
            vmem((2 * S, N * H), BF),
            vmem((B, B), BF),
            vmem((N * B, B), BF),
            vmem((N * B, N * B), BF),
            vmem((N * B, N * B), BF),
            vmem((N * B, N * B), BF),
            vmem((2 * B, N * B), BF),
            vmem((2 * B, N * B), BF),
            vmem((2 * B, N * B), BF),
            vmem((2 * B, N * B), BF),
            vmem((2 * B, N * B), BF),
            vmem((2 * B, 4 * B), F32),
            vmem((N * B, B), BF),
            vmem((2 * B, B), BF),
            dma((4,)), dma((4,)), dma((4, 4)), dma((4, 4)), dma((4, 2)), dma((4, 2)),
            dma((3,)), dma((3, 3)), dma((3,)), dma((3,)),
            dma(()), dma(()), dma((2,)), dma(()), dma((3, 2, 4)), dma((3, 2, 4)), dma((4, 4)), dma((4, 4)),
            dma((3,)), dma((3,)), dma((4,)), dma((4,)), dma(()), dma(()), dma((2,)), dma(()),
            dma((4,)), dma((10,)),
        ],
        compiler_params=pltpu.CompilerParams(
            has_side_effects=True, collective_id=0, vmem_limit_bytes=58 * 2**20
        ),
        name="fused",
    )(live, win, inv, pan, trail)


def hand_out_kernel(pan, win, trail, pan_out, win_out, trail_out, pv, wv, tv, load, store):
    parts = [(pan, pv, pan_out, 0, 512)]
    parts += [(win, wv, win_out, i * 1024, 1024) for i in range(2)]
    parts += [(trail, tv, trail_out, i * 128, 128) for i in range(4)]

    def move(n, inward):
        src, mid, dst, first, count = parts[n]
        at = slice(first, first + count)
        if inward:
            return pltpu.make_async_copy(src.at[at, :], mid.at[at, :], load.at[n])
        return pltpu.make_async_copy(mid.at[at, :], dst.at[at, :], store.at[n])

    for n in range(len(parts)):
        move(n, True).start()
    for n in range(len(parts)):
        move(n, True).wait()
        move(n, False).start()
    for n in range(len(parts)):
        move(n, False).wait()


def hand_out(*arrays):
    anys = pl.BlockSpec(memory_space=pl.ANY)
    dma = pltpu.SemaphoreType.DMA
    return pl.pallas_call(
        hand_out_kernel,
        out_shape=tuple(jax.ShapeDtypeStruct(a.shape, a.dtype) for a in arrays),
        in_specs=[anys] * 3,
        out_specs=(anys,) * 3,
        scratch_shapes=[pltpu.VMEM(a.shape, a.dtype) for a in arrays] + [dma((7,)), dma((7,))],
        name="hand_out",
    )(*arrays)


def local_part(panel_blocks, live_rows, window_blocks, diag_inverse, trailing):
    return hand_out(*fused(live_rows, window_blocks, diag_inverse[0], panel_blocks, trailing))


def solution(mesh):
    return jax.shard_map(
        local_part,
        mesh=mesh,
        in_specs=(
            P("row", "col"),
            P("col", "row"),
            P(None, "col"),
            P("col", None, None),
            P("row", "col"),
        ),
        out_specs=(P("row", "col"), P(None, "col"), P("row", "col")),
        check_vma=False,
    )
```

```python
import jax
import jax.numpy as jnp
from jax import lax
from jax.experimental import pallas as pl
from jax.experimental.pallas import tpu as pltpu
from jax.sharding import PartitionSpec as P

B = 256
S = 16
H = 128
N = 8
BF = jnp.bfloat16
F32 = jnp.float32
MESH = pl.DeviceIdType.MESH


def place():
    row = lax.axis_index("row")
    col = lax.axis_index("col")
    return row, col, col // 2, row % 4, row // 4, col % 2


def bits_of(y, z):
    return [((y + 1) // 2) % 2, ((z + 1) // 2) % 2, y // 2, z // 2]


def address(bits, k):
    return sum(bits[(k + i) % 4] * 2**i for i in range(4))


def partners(y, z):
    ya = y + 1 - 2 * (y % 2)
    za = z + 1 - 2 * (z % 2)
    return [z * 4 + ya, za * 4 + y, z * 4 + 3 - y, (3 - z) * 4 + y]


def pick(a, b, c):
    return a * (1 - c) + b * c


def lanes(c):
    return pl.ds(pl.multiple_of(c * B, B), B)


def rows(start, count):
    return pl.ds(pl.multiple_of(start, S), count)


def lane(p):
    return slice(p * B, p * B + B)


def nt(a, b):
    return lax.dot_general(a, b, (((1,), (1,)), ((), ())), preferred_element_type=F32)


def kernel(
    live, win, inv, pan, trail, pan_out, win_out, trail_out,
    pv, pp, st, a0, kp, krow, kcol, iv, wc, wg, wf, u, ar, fr, am, fm, ao, tr, wo, po,
    wx_recv, wx_send, wh_recv, wh_send, wd_recv, wd_send, wr_recv, wr_send, we_recv, we_send,
    a1_recv, a1_send, a2_recv, a2_send, ah_recv, ah_send, a3_recv, a3_send,
    ar_recv, ar_send, ad_recv, ad_send, kr_recv, kr_send, kc_recv, kc_send, lsem, osem,
):
    row, col, x, y, z, core = place()
    bits = bits_of(y, z)
    addr = [address(bits, k) for k in range(4)]
    near = partners(y, z)
    other = 1 - core
    h = y % 2
    sibling = x * 2 + other
    own = (z == x) & (y // 2 == core)

    def local(src, dst, sem):
        return pltpu.make_async_copy(src, dst, sem)

    def take(ref, sem):
        pltpu.make_async_copy(ref, ref, sem).wait()

    def remote(src, dst, ssem, rsem, r, c):
        return pltpu.make_async_remote_copy(
            src_ref=src, dst_ref=dst, send_sem=ssem, recv_sem=rsem, device_id=(r, c), device_id_type=MESH
        )

    load = local(pan, pv, lsem.at[0])
    load.start()
    load_window = local(win, wc, lsem.at[1])
    load_window.start()
    load_inverse = local(inv, iv, lsem.at[3])
    load_inverse.start()
    load_trail = local(trail, tr, lsem.at[2])
    load_trail.start()

    barrier = pltpu.get_barrier_semaphore()

    def greet(r, c):
        pl.semaphore_signal(barrier, inc=1, device_id=(r, c), device_id_type=MESH)

    for d in range(1, 8):
        greet(row, (col + d) % 8)
    for d in range(1, 16):
        greet((row + d) % 16, col)

    l0 = live[0, 0]
    l1 = live[0, 1]
    load.wait()
    pv[B : 2 * B, :] = jnp.where(l0 == 1, pv[0:B, :], pv[B : 2 * B, :])
    keep0 = jnp.where(l0 == 0, 1.0, 0.0)
    keep1 = jnp.where((l0 == 1) | (l1 == 1), 1.0, 0.0)
    kp[...] = jnp.where(lax.broadcasted_iota(jnp.int32, (S, H), 0) == 0, keep0, keep1).astype(BF)
    for t in range(16):
        tbits = bits_of(t % 4, t // 4)
        for kk in range(2):
            s = pick(address(tbits, kk), address(tbits, 2 + kk), h)
            pp[t * 2 * S + kk * S : t * 2 * S + kk * S + S, :] = pv[rows(kk * B + s * S, S), :]

    pl.semaphore_wait(barrier, 22)

    mine = st.at[rows(row * 2 * S, 2 * S), :]
    local(pp.at[rows(row * 2 * S, 2 * S), :], mine, a1_recv).start()

    def scatter(d, carry):
        t = (row + d) % 16
        remote(pp.at[rows(t * 2 * S, 2 * S), :], mine, a1_send, a1_recv, t, col).start()
        return carry

    lax.fori_loop(1, 16, scatter, 0)

    load_window.wait()
    load_inverse.wait()
    wc[lanes(col), :] = iv[...]
    for j in range(4):

        @pl.when(x <= (0, 1, 0, 2)[j])
        def _():
            for kc in range(2):
                t = addr[j] if kc == 0 else addr[3 - j]
                at = rows((2 * j + kc) * B + t * S, S)
                src = wc.at[at, :]
                dst = wg.at[at, lanes(col)]
                for d in range(4):
                    target = (x + d) % 4 * 2 + kc
                    if d == 0:

                        @pl.when(core == kc)
                        def _():
                            local(src, dst, wx_recv.at[j]).start()

                        @pl.when(core != kc)
                        def _():
                            remote(src, dst, wx_send.at[j], wx_recv.at[j], row, target).start()
                    else:
                        remote(src, dst, wx_send.at[j], wx_recv.at[j], row, target).start()

    def w_width(j):
        return (2, 4, 2, 6)[j] * B

    def w_base(j, i):
        n = 2**i
        return pick(addr[j], addr[3 - j], core) // n * n

    def w_part(j, base, n, c):
        return wg.at[rows((2 * j + c) * B + base * S, n * S), pl.ds(0, w_width(j))]

    def w_got(j, i):
        n = 2**i
        a = pick(addr[j], addr[3 - j], core)
        return w_part(j, a // (2 * n) * (2 * n) + (1 - a // n % 2) * n, n, core)

    def w_step(i):
        for j in range(4):
            if i == 0:
                take(w_part(j, w_base(j, 0), 1, core), wx_recv.at[j])
            else:
                take(w_got(j, i - 1), wh_recv.at[i - 1, j])
            part = w_part(j, w_base(j, i), 2**i, core)
            to = pick(near[(j + i) % 4], near[(3 - j + i) % 4], core)
            remote(part, part, wh_send.at[i, j], wh_recv.at[i, j], to, col).start()
            if i == 3:
                remote(part, part, wd_send.at[j, 0], wd_recv.at[j, 0], row, sibling).start()

    def a_part(k, base, n, g):
        return am.at[rows(k * H + base * S, n * S), slice(g * 4 * B, g * 4 * B + 4 * B)]

    def a_got(k, i, g):
        n = 2**i
        a = addr[k] % 8
        return a_part(k, a // (2 * n) * (2 * n) + (1 - a // n % 2) * n, n, g)

    def a_step(i, g):
        n = 2**i
        chunk = slice(g * 4 * B, g * 4 * B + 4 * B)
        if i == 0:
            take(a0.at[:, chunk], a2_recv.at[g])
            for k in range(4):
                am[rows(k * H + addr[k] % 8 * S, S), chunk] = a0[k * S : k * S + S, chunk]
        for k in range(4):
            if i > 0:
                take(a_got(k, i - 1, g), ah_recv.at[i - 1, g, k])
            if i < 3:
                part = a_part(k, addr[k] % 8 // n * n, n, g)
                remote(part, part, ah_send.at[i, g, k], ah_recv.at[i, g, k], near[(k + i) % 4], col).start()

    def a_last(g):
        for k in range(4):
            there = slice(k * H, k * H + H), slice(g * 2 * B, g * 2 * B + 2 * B)
            remote(fm.at[there], ao.at[there], a3_send.at[g, k], a3_recv.at[g, k], near[(k + 3) % 4], col).start()

    pieces = [(1, 0), (2, 0), (3, 1)]

    def piece(n, c):
        xs, hf = pieces[n]
        return (4 + 2 * hf) * B, lanes(2 * xs + c)

    def whole_send(n):
        xs, hf = pieces[n]

        @pl.when(x == xs)
        def _():
            first, at = piece(n, core)
            src = wc.at[first : first + 2 * B, :]
            dst = wg.at[first : first + 2 * B, at]
            local(src, dst, wr_recv.at[n]).start()
            for d in range(1, 4):
                remote(src, dst, wr_send.at[n, d - 1], wr_recv.at[n], row, (x + d) % 4 * 2 + core).start()

    def whole_share(n):
        xs, hf = pieces[n]
        first, at = piece(n, core)
        got = wg.at[first : first + 2 * B, at]
        take(got, wr_recv.at[n])
        remote(got, got, we_send.at[n], we_recv.at[n], row, sibling).start()

    def whole_take(n):
        first, at = piece(n, other)
        take(wg.at[first : first + 2 * B, at], we_recv.at[n])

    w_step(0)
    take(st, a1_recv)
    for d in range(4):
        xd = (x + d) % 4
        for kc in range(2):
            src = st.at[rows((4 * xd + 2 * kc) * 2 * S, 4 * S), :]
            dst = a0.at[:, lanes(col)]
            if d == 0:

                @pl.when(core == kc)
                def _():
                    local(src, dst, a2_recv.at[x // 2]).start()

                @pl.when(core != kc)
                def _():
                    remote(src, dst, a2_send, a2_recv.at[x // 2], row, sibling).start()
            else:
                remote(src, dst, a2_send, a2_recv.at[x // 2], row, xd * 2 + kc).start()

    w_step(1)
    kept = krow.at[:, pl.ds(pl.multiple_of(col * H, H), H)]
    local(kp, kept, kr_recv).start()
    for d in range(1, 8):
        remote(kp, kept, kr_send, kr_recv, row, (col + d) % 8).start()
    for n in range(len(pieces)):
        whole_send(n)
    a_step(0, 0)
    a_step(0, 1)
    w_step(2)
    w_step(3)
    panel = ar.at[:, lanes(col)]
    local(pv, panel, lsem.at[0]).start()
    for d in range(1, 4):
        remote(pv, panel, ar_send.at[d - 1], ar_recv.at[d - 1], row, (x + d) % 4 * 2 + core).start()
    remote(pv, panel, ad_send.at[0], ad_recv.at[0], row, sibling).start()

    a_step(1, 0)
    a_step(1, 1)
    take(krow, kr_recv)

    @pl.when(own)
    def _():
        dst = kcol.at[rows(h * S, S), :]
        local(krow, dst, kc_recv.at[h]).start()
        for d in range(1, 16):
            remote(krow, dst, kc_send, kc_recv.at[h], (row + d) % 16, col).start()

    for j in range(4):
        got = w_got(j, 3)
        take(got, wh_recv.at[3, j])
        remote(got, got, wd_send.at[j, 1], wd_recv.at[j, 1], row, sibling).start()
    a_step(2, 0)
    a_step(2, 1)
    for n in range(len(pieces)):
        whole_share(n)
    for j in range(4):
        a = pick(addr[3 - j], addr[j], core) // 8
        take(w_part(j, a * 8, 8, other), wd_recv.at[j, 0])
        take(w_part(j, (1 - a) * 8, 8, other), wd_recv.at[j, 1])

    def keep(ref, first, i, p):
        t = ref[first : first + S, p * H : p * H + H].astype(F32)[i : i + 1, :]
        return jnp.concatenate([t, t], axis=1) > 0.5

    def masked(value, mask):
        return jnp.where(mask, value, 0.0).astype(BF)

    def operand(factors, raw, at, p):
        if p == 0:
            return raw[at, lane(p)]
        return jnp.concatenate([factors[at, : p * B], raw[at, lane(p)]], axis=1)

    take(kcol.at[0:S, :], kc_recv.at[0])
    take(kcol.at[S : 2 * S, :], kc_recv.at[1])

    def solve(p, factors, raw):
        up = u[lane(p), : (p + 1) * B]
        out = nt(operand(factors, raw, slice(0, 2 * B), p), up)
        for k in range(4):
            part = slice(k * H, k * H + H)
            factors[part, lane(p)] = masked(out[part, :], keep(kcol, k // 2 * S, k % 2, p))

    for p in range(N):
        if p == 2:
            whole_take(0)
        if p == 4:
            whole_take(1)
        if p == 6:
            whole_take(2)
        diag = wg[lane(p), lane(p)]
        if p > 0:
            prev = jnp.dot(diag, wf[lane(p), : p * B], preferred_element_type=F32)
            u[lane(p), : p * B] = (-prev).astype(BF)
        u[lane(p), lane(p)] = diag
        up = u[lane(p), : (p + 1) * B]
        for q in range(p + 1, N):
            wf[lane(q), lane(p)] = nt(operand(wf, wg, lane(q), p), up).astype(BF)
        if p == 4:
            a_step(3, 0)
        if p == 6:
            a_step(3, 1)
        for p2 in ((), (), (), (), (0, 1), (2, 3), (4, 5), (6, 7))[p]:
            solve(p2, fm, am)
            if p2 % 2 == 1:
                a_last(p2 // 2)

    here = lanes(col)
    for q in range(N):
        block = wf[lane(q), here]
        wo[lane(q), :] = jnp.where(q > col, block, jnp.zeros_like(block))
    local(wo, win_out, osem.at[0]).start()

    def update(factors, far, first, last):
        for g in range(2):
            prod = nt(fr[:, first:last], factors[lane(g), first:last])
            for e in range(2):
                k = 2 * g + e
                half = addr[k] // 8
                if far:
                    half = 1 - half
                at = pl.ds(pl.multiple_of(k * B + half * H, H), H)
                tr[:, at] = tr[:, at] - prod[:, e * H : e * H + H]
                if last == N * B:
                    local(tr.at[:, at], trail_out.at[:, at], osem.at[2 + 4 * far + k]).start()

    def take_far(g):
        for k in range(4):
            take(ao.at[k * H : k * H + H, g * 2 * B : g * 2 * B + 2 * B], a3_recv.at[g, k])

    for d in range(1, 4):
        got = ar.at[:, lanes((x + 4 - d) % 4 * 2 + core)]
        take(got, ar_recv.at[d - 1])
        remote(got, got, ad_send.at[d], ad_recv.at[d], row, sibling).start()
    local(pv, panel, lsem.at[0]).wait()
    for d in range(4):
        take(ar.at[:, lanes((x + 4 - d) % 4 * 2 + other)], ad_recv.at[d])
    for p in range(N):
        up = u[lane(p), : (p + 1) * B]
        for i in range(2):
            fr[lane(i), lane(p)] = masked(nt(operand(fr, ar, lane(i), p), up), keep(krow, 0, i, p))
    f0 = fr[0:B, here]
    f1 = fr[B : 2 * B, here]
    po[0:B, :] = jnp.where(l0 == 0, f0, f1)
    po[B : 2 * B, :] = jnp.where(l0 == 0, f1, jnp.zeros_like(f1))
    local(po, pan_out, osem.at[1]).start()

    load_trail.wait()
    update(fm, 0, 0, N * B)

    for g in range(3):
        take_far(g)
    update(ao, 1, 0, 6 * B)
    take_far(3)
    update(ao, 1, 6 * B, N * B)

    for j in range(4):

        @pl.when(x <= (0, 1, 0, 2)[j])
        def _():
            take(pv.at[pl.ds(0, 7 * S), :], wx_send.at[j])

        for i in range(4):
            take(w_part(j, w_base(j, i), 2**i, core), wh_send.at[i, j])
        take(w_part(j, w_base(j, 3), 8, core), wd_send.at[j, 0])
        take(w_got(j, 3), wd_send.at[j, 1])
        for i in range(3):
            n = 2**i
            for g in range(2):
                take(a_part(j, addr[j] % 8 // n * n, n, g), ah_send.at[i, g, j])
        for g in range(4):
            take(fm.at[j * H : j * H + H, g * 2 * B : g * 2 * B + 2 * B], a3_send.at[g, j])
    take(pv.at[pl.ds(0, 15 * 2 * S), :], a1_send)
    take(pv.at[pl.ds(0, 7 * 4 * S), :], a2_send)
    for n in range(len(pieces)):
        xs, hf = pieces[n]
        take(pv, we_send.at[n])

        @pl.when(x == xs)
        def _():
            for d in range(3):
                take(pv, wr_send.at[n, d])

    for d in range(4):
        take(pv, ad_send.at[d])
        if d < 3:
            take(pv, ar_send.at[d])
    take(krow.at[:, 0 : 7 * H], kr_send)

    @pl.when(own)
    def _():
        take(ar.at[0 : 15 * S, 0 : N * H], kc_send)

    local(wo, win_out, osem.at[0]).wait()
    local(po, pan_out, osem.at[1]).wait()
    for far in range(2):
        for k in range(4):
            half = addr[k] // 8
            if far:
                half = 1 - half
            at = pl.ds(pl.multiple_of(k * B + half * H, H), H)
            local(tr.at[:, at], trail_out.at[:, at], osem.at[2 + 4 * far + k]).wait()


def fused(live, win, inv, pan, trail):
    dma = pltpu.SemaphoreType.DMA
    anys = pl.BlockSpec(memory_space=pl.ANY)
    smem = pl.BlockSpec(memory_space=pltpu.SMEM)
    vmem = pltpu.VMEM
    return pl.pallas_call(
        kernel,
        out_shape=(
            jax.ShapeDtypeStruct((2 * B, B), BF),
            jax.ShapeDtypeStruct((N * B, B), BF),
            jax.ShapeDtypeStruct((2 * B, 4 * B), F32),
        ),
        in_specs=[smem] + [anys] * 4,
        out_specs=(anys,) * 3,
        scratch_shapes=[
            vmem((2 * B, B), BF),
            vmem((2 * B, B), BF),
            vmem((2 * B, B), BF),
            vmem((4 * S, N * B), BF),
            vmem((S, H), BF),
            vmem((S, N * H), BF),
            vmem((2 * S, N * H), BF),
            vmem((B, B), BF),
            vmem((N * B, B), BF),
            vmem((N * B, N * B), BF),
            vmem((N * B, N * B), BF),
            vmem((N * B, N * B), BF),
            vmem((2 * B, N * B), BF),
            vmem((2 * B, N * B), BF),
            vmem((2 * B, N * B), BF),
            vmem((2 * B, N * B), BF),
            vmem((2 * B, N * B), BF),
            vmem((2 * B, 4 * B), F32),
            vmem((N * B, B), BF),
            vmem((2 * B, B), BF),
            dma((4,)), dma((4,)), dma((4, 4)), dma((4, 4)), dma((4, 2)), dma((4, 2)),
            dma((3,)), dma((3, 3)), dma((3,)), dma((3,)),
            dma(()), dma(()), dma((2,)), dma(()), dma((3, 2, 4)), dma((3, 2, 4)), dma((4, 4)), dma((4, 4)),
            dma((3,)), dma((3,)), dma((4,)), dma((4,)), dma(()), dma(()), dma((2,)), dma(()),
            dma((4,)), dma((10,)),
        ],
        compiler_params=pltpu.CompilerParams(
            has_side_effects=True, collective_id=0, vmem_limit_bytes=58 * 2**20
        ),
        name="fused",
    )(live, win, inv, pan, trail)


def hand_out_kernel(pan, win, trail, pan_out, win_out, trail_out, pv, wv, tv, load, store):
    parts = [(pan, pv, pan_out, 0, 512)]
    parts += [(win, wv, win_out, i * 1024, 1024) for i in range(2)]
    parts += [(trail, tv, trail_out, i * 128, 128) for i in range(4)]

    def move(n, inward):
        src, mid, dst, first, count = parts[n]
        at = slice(first, first + count)
        if inward:
            return pltpu.make_async_copy(src.at[at, :], mid.at[at, :], load.at[n])
        return pltpu.make_async_copy(mid.at[at, :], dst.at[at, :], store.at[n])

    for n in range(len(parts)):
        move(n, True).start()
    for n in range(len(parts)):
        move(n, True).wait()
        move(n, False).start()
    for n in range(len(parts)):
        move(n, False).wait()


def hand_out(*arrays):
    anys = pl.BlockSpec(memory_space=pl.ANY)
    dma = pltpu.SemaphoreType.DMA
    return pl.pallas_call(
        hand_out_kernel,
        out_shape=tuple(jax.ShapeDtypeStruct(a.shape, a.dtype) for a in arrays),
        in_specs=[anys] * 3,
        out_specs=(anys,) * 3,
        scratch_shapes=[pltpu.VMEM(a.shape, a.dtype) for a in arrays] + [dma((7,)), dma((7,))],
        name="hand_out",
    )(*arrays)


def local_part(panel_blocks, live_rows, window_blocks, diag_inverse, trailing):
    return hand_out(*fused(live_rows, window_blocks, diag_inverse[0], panel_blocks, trailing))


def solution(mesh):
    return jax.shard_map(
        local_part,
        mesh=mesh,
        in_specs=(
            P("row", "col"),
            P("col", "row"),
            P(None, "col"),
            P("col", None, None),
            P("row", "col"),
        ),
        out_specs=(P("row", "col"), P(None, "col"), P("row", "col")),
        check_vma=False,
    )
```

```python
import jax
import jax.numpy as jnp
from jax import lax
from jax.experimental import pallas as pl
from jax.experimental.pallas import tpu as pltpu
from jax.sharding import PartitionSpec as P

B = 256
S = 16
H = 128
N = 8
BF = jnp.bfloat16
F32 = jnp.float32
MESH = pl.DeviceIdType.MESH


def place():
    row = lax.axis_index("row")
    col = lax.axis_index("col")
    return row, col, col // 2, row % 4, row // 4, col % 2


def bits_of(y, z):
    return [((y + 1) // 2) % 2, ((z + 1) // 2) % 2, y // 2, z // 2]


def address(bits, k):
    return sum(bits[(k + i) % 4] * 2**i for i in range(4))


def partners(y, z):
    ya = y + 1 - 2 * (y % 2)
    za = z + 1 - 2 * (z % 2)
    return [z * 4 + ya, za * 4 + y, z * 4 + 3 - y, (3 - z) * 4 + y]


def pick(a, b, c):
    return a * (1 - c) + b * c


def lanes(c):
    return pl.ds(pl.multiple_of(c * B, B), B)


def rows(start, count):
    return pl.ds(pl.multiple_of(start, S), count)


def lane(p):
    return slice(p * B, p * B + B)


def nt(a, b):
    return lax.dot_general(a, b, (((1,), (1,)), ((), ())), preferred_element_type=F32)


def kernel(
    live, win, inv, pan, trail, pan_out, win_out, trail_out,
    pv, pp, st, a0, kp, krow, kf, kcol, iv, wc, wg, wf, u, ar, fr, am, fm, ao, tr, wo, po,
    wx_recv, wx_send, wh_recv, wh_send, wd_recv, wd_send, wr_recv, wr_send, we_recv, we_send,
    a1_recv, a1_send, a2_recv, a2_send, ah_recv, ah_send, a3_recv, a3_send,
    ar_recv, ar_send, ad_recv, ad_send, kr_recv, kr_send, kc_recv, kc_send, lsem, osem,
):
    row, col, x, y, z, core = place()
    bits = bits_of(y, z)
    addr = [address(bits, k) for k in range(4)]
    near = partners(y, z)
    other = 1 - core
    h = y % 2
    sibling = x * 2 + other
    own = (z == x) & (y // 2 == core)

    def local(src, dst, sem):
        return pltpu.make_async_copy(src, dst, sem)

    def take(ref, sem):
        pltpu.make_async_copy(ref, ref, sem).wait()

    def remote(src, dst, ssem, rsem, r, c):
        return pltpu.make_async_remote_copy(
            src_ref=src, dst_ref=dst, send_sem=ssem, recv_sem=rsem, device_id=(r, c), device_id_type=MESH
        )

    load = local(pan, pv, lsem.at[0])
    load.start()
    load_window = local(win, wc, lsem.at[1])
    load_window.start()
    load_inverse = local(inv, iv, lsem.at[3])
    load_inverse.start()
    load_trail = local(trail, tr, lsem.at[2])
    load_trail.start()

    barrier = pltpu.get_barrier_semaphore()

    def greet(r, c):
        pl.semaphore_signal(barrier, inc=1, device_id=(r, c), device_id_type=MESH)

    for d in range(1, 8):
        greet(row, (col + d) % 8)
    for d in range(1, 16):
        greet((row + d) % 16, col)

    l0 = live[0, 0]
    l1 = live[0, 1]
    load.wait()
    pv[B : 2 * B, :] = jnp.where(l0 == 1, pv[0:B, :], pv[B : 2 * B, :])
    keep0 = jnp.where(l0 == 0, 1.0, 0.0)
    keep1 = jnp.where((l0 == 1) | (l1 == 1), 1.0, 0.0)
    kp[...] = jnp.where(lax.broadcasted_iota(jnp.int32, (S, H), 0) == 0, keep0, keep1).astype(BF)
    for t in range(16):
        tbits = bits_of(t % 4, t // 4)
        for kk in range(2):
            s = pick(address(tbits, kk), address(tbits, 2 + kk), h)
            pp[t * 2 * S + kk * S : t * 2 * S + kk * S + S, :] = pv[rows(kk * B + s * S, S), :]

    pl.semaphore_wait(barrier, 22)

    mine = st.at[rows(row * 2 * S, 2 * S), :]
    local(pp.at[rows(row * 2 * S, 2 * S), :], mine, a1_recv).start()

    def scatter(d, carry):
        t = (row + d) % 16
        remote(pp.at[rows(t * 2 * S, 2 * S), :], mine, a1_send, a1_recv, t, col).start()
        return carry

    lax.fori_loop(1, 16, scatter, 0)

    kept = krow.at[:, pl.ds(pl.multiple_of(col * H, H), H)]
    local(kp, kept, kr_recv).start()
    for d in range(1, 8):
        remote(kp, kept, kr_send, kr_recv, row, (col + d) % 8).start()
    load_window.wait()
    load_inverse.wait()
    wc[lanes(col), :] = iv[...]
    for j in range(4):

        @pl.when(x <= (0, 1, 0, 2)[j])
        def _():
            for kc in range(2):
                t = addr[j] if kc == 0 else addr[3 - j]
                at = rows((2 * j + kc) * B + t * S, S)
                src = wc.at[at, :]
                dst = wg.at[at, lanes(col)]
                for d in range(4):
                    target = (x + d) % 4 * 2 + kc
                    if d == 0:

                        @pl.when(core == kc)
                        def _():
                            local(src, dst, wx_recv.at[j]).start()

                        @pl.when(core != kc)
                        def _():
                            remote(src, dst, wx_send.at[j], wx_recv.at[j], row, target).start()
                    else:
                        remote(src, dst, wx_send.at[j], wx_recv.at[j], row, target).start()

    def w_width(j):
        return (2, 4, 2, 6)[j] * B

    def w_base(j, i):
        n = 2**i
        return pick(addr[j], addr[3 - j], core) // n * n

    def w_part(j, base, n, c):
        return wg.at[rows((2 * j + c) * B + base * S, n * S), pl.ds(0, w_width(j))]

    def w_got(j, i):
        n = 2**i
        a = pick(addr[j], addr[3 - j], core)
        return w_part(j, a // (2 * n) * (2 * n) + (1 - a // n % 2) * n, n, core)

    def w_step(i):
        for j in range(4):
            if i == 0:
                take(w_part(j, w_base(j, 0), 1, core), wx_recv.at[j])
            else:
                take(w_got(j, i - 1), wh_recv.at[i - 1, j])
            part = w_part(j, w_base(j, i), 2**i, core)
            to = pick(near[(j + i) % 4], near[(3 - j + i) % 4], core)
            remote(part, part, wh_send.at[i, j], wh_recv.at[i, j], to, col).start()
            if i == 3:
                remote(part, part, wd_send.at[j, 0], wd_recv.at[j, 0], row, sibling).start()

    def a_part(k, base, n, g):
        return am.at[rows(k * H + base * S, n * S), slice(g * 4 * B, g * 4 * B + 4 * B)]

    def a_got(k, i, g):
        n = 2**i
        a = addr[k] % 8
        return a_part(k, a // (2 * n) * (2 * n) + (1 - a // n % 2) * n, n, g)

    def a_step(i, g):
        n = 2**i
        chunk = slice(g * 4 * B, g * 4 * B + 4 * B)
        if i == 0:
            take(a0.at[:, chunk], a2_recv.at[g])
            for k in range(4):
                am[rows(k * H + addr[k] % 8 * S, S), chunk] = a0[k * S : k * S + S, chunk]
        for k in range(4):
            if i > 0:
                take(a_got(k, i - 1, g), ah_recv.at[i - 1, g, k])
            if i < 3:
                part = a_part(k, addr[k] % 8 // n * n, n, g)
                remote(part, part, ah_send.at[i, g, k], ah_recv.at[i, g, k], near[(k + i) % 4], col).start()

    def a_last(g):
        for k in range(4):
            there = slice(k * H, k * H + H), slice(g * 2 * B, g * 2 * B + 2 * B)
            remote(fm.at[there], ao.at[there], a3_send.at[g, k], a3_recv.at[g, k], near[(k + 3) % 4], col).start()

    pieces = [(1, 0), (2, 0), (3, 1)]

    def piece(n, c):
        xs, hf = pieces[n]
        return (4 + 2 * hf) * B, lanes(2 * xs + c)

    def whole_send(n):
        xs, hf = pieces[n]

        @pl.when(x == xs)
        def _():
            first, at = piece(n, core)
            src = wc.at[first : first + 2 * B, :]
            dst = wg.at[first : first + 2 * B, at]
            local(src, dst, wr_recv.at[n]).start()
            for d in range(1, 4):
                remote(src, dst, wr_send.at[n, d - 1], wr_recv.at[n], row, (x + d) % 4 * 2 + core).start()

    def whole_share(n):
        xs, hf = pieces[n]
        first, at = piece(n, core)
        got = wg.at[first : first + 2 * B, at]
        take(got, wr_recv.at[n])
        remote(got, got, we_send.at[n], we_recv.at[n], row, sibling).start()

    def whole_take(n):
        first, at = piece(n, other)
        take(wg.at[first : first + 2 * B, at], we_recv.at[n])

    w_step(0)
    take(st, a1_recv)
    for d in range(4):
        xd = (x + d) % 4
        for kc in range(2):
            src = st.at[rows((4 * xd + 2 * kc) * 2 * S, 4 * S), :]
            dst = a0.at[:, lanes(col)]
            if d == 0:

                @pl.when(core == kc)
                def _():
                    local(src, dst, a2_recv.at[x // 2]).start()

                @pl.when(core != kc)
                def _():
                    remote(src, dst, a2_send, a2_recv.at[x // 2], row, sibling).start()
            else:
                remote(src, dst, a2_send, a2_recv.at[x // 2], row, xd * 2 + kc).start()

    w_step(1)
    take(krow, kr_recv)
    at_row = lax.broadcasted_iota(jnp.int32, (S, H), 0)
    flags = jnp.zeros((S, H), F32)
    for p in range(N):
        two = krow[:, p * H : p * H + H].astype(F32)
        for i in range(2):
            flags = jnp.where(at_row == 2 * p + i, two[i : i + 1, :], flags)
    kf[...] = flags.astype(BF)

    @pl.when(own)
    def _():
        dst = kcol.at[rows(h * S, S), :]
        local(kf, dst, kc_recv.at[h]).start()
        for d in range(1, 16):
            remote(kf, dst, kc_send, kc_recv.at[h], (row + d) % 16, col).start()

    a_step(0, 0)
    a_step(0, 1)
    for n in range(len(pieces)):
        whole_send(n)
    w_step(2)
    w_step(3)
    panel = ar.at[:, lanes(col)]
    local(pv, panel, lsem.at[0]).start()
    for d in range(1, 4):
        remote(pv, panel, ar_send.at[d - 1], ar_recv.at[d - 1], row, (x + d) % 4 * 2 + core).start()
    remote(pv, panel, ad_send.at[0], ad_recv.at[0], row, sibling).start()

    a_step(1, 0)
    a_step(1, 1)
    for j in range(4):
        got = w_got(j, 3)
        take(got, wh_recv.at[3, j])
        remote(got, got, wd_send.at[j, 1], wd_recv.at[j, 1], row, sibling).start()
    a_step(2, 0)
    a_step(2, 1)
    for n in range(len(pieces)):
        whole_share(n)
    for j in range(4):
        a = pick(addr[3 - j], addr[j], core) // 8
        take(w_part(j, a * 8, 8, other), wd_recv.at[j, 0])
        take(w_part(j, (1 - a) * 8, 8, other), wd_recv.at[j, 1])

    def keep(ref, first, i, p):
        t = ref[first : first + S, :].astype(F32)[2 * p + i : 2 * p + i + 1, :]
        return jnp.concatenate([t, t], axis=1) > 0.5

    def masked(value, mask):
        return jnp.where(mask, value, 0.0).astype(BF)

    def operand(factors, raw, at, p):
        if p == 0:
            return raw[at, lane(p)]
        return jnp.concatenate([factors[at, : p * B], raw[at, lane(p)]], axis=1)

    take(kcol.at[0:S, :], kc_recv.at[0])
    take(kcol.at[S : 2 * S, :], kc_recv.at[1])

    def solve(p, factors, raw):
        up = u[lane(p), : (p + 1) * B]
        out = nt(operand(factors, raw, slice(0, 2 * B), p), up)
        for k in range(4):
            part = slice(k * H, k * H + H)
            factors[part, lane(p)] = masked(out[part, :], keep(kcol, k // 2 * S, k % 2, p))

    for p in range(N):
        if p == 2:
            whole_take(0)
        if p == 4:
            whole_take(1)
        if p == 6:
            whole_take(2)
        diag = wg[lane(p), lane(p)]
        if p > 0:
            prev = jnp.dot(diag, wf[lane(p), : p * B], preferred_element_type=F32)
            u[lane(p), : p * B] = (-prev).astype(BF)
        u[lane(p), lane(p)] = diag
        up = u[lane(p), : (p + 1) * B]
        for q in range(p + 1, N):
            wf[lane(q), lane(p)] = nt(operand(wf, wg, lane(q), p), up).astype(BF)
        if p == 4:
            a_step(3, 0)
        if p == 6:
            a_step(3, 1)
        for p2 in ((), (), (), (), (0, 1), (2, 3), (4, 5), (6, 7))[p]:
            solve(p2, fm, am)
            if p2 % 2 == 1:
                a_last(p2 // 2)

    here = lanes(col)
    for q in range(N):
        block = wf[lane(q), here]
        wo[lane(q), :] = jnp.where(q > col, block, jnp.zeros_like(block))
    local(wo, win_out, osem.at[0]).start()

    def update(factors, far, first, last):
        for g in range(2):
            prod = nt(fr[:, first:last], factors[lane(g), first:last])
            for e in range(2):
                k = 2 * g + e
                half = addr[k] // 8
                if far:
                    half = 1 - half
                at = pl.ds(pl.multiple_of(k * B + half * H, H), H)
                tr[:, at] = tr[:, at] - prod[:, e * H : e * H + H]
                if last == N * B:
                    local(tr.at[:, at], trail_out.at[:, at], osem.at[2 + 4 * far + k]).start()

    def take_far(g):
        for k in range(4):
            take(ao.at[k * H : k * H + H, g * 2 * B : g * 2 * B + 2 * B], a3_recv.at[g, k])

    for d in range(1, 4):
        got = ar.at[:, lanes((x + 4 - d) % 4 * 2 + core)]
        take(got, ar_recv.at[d - 1])
        remote(got, got, ad_send.at[d], ad_recv.at[d], row, sibling).start()
    local(pv, panel, lsem.at[0]).wait()
    for d in range(4):
        take(ar.at[:, lanes((x + 4 - d) % 4 * 2 + other)], ad_recv.at[d])
    for p in range(N):
        up = u[lane(p), : (p + 1) * B]
        for i in range(2):
            fr[lane(i), lane(p)] = masked(nt(operand(fr, ar, lane(i), p), up), keep(kf, 0, i, p))
    f0 = fr[0:B, here]
    f1 = fr[B : 2 * B, here]
    po[0:B, :] = jnp.where(l0 == 0, f0, f1)
    po[B : 2 * B, :] = jnp.where(l0 == 0, f1, jnp.zeros_like(f1))
    local(po, pan_out, osem.at[1]).start()

    load_trail.wait()
    update(fm, 0, 0, N * B)

    for g in range(3):
        take_far(g)
    update(ao, 1, 0, 6 * B)
    take_far(3)
    update(ao, 1, 6 * B, N * B)

    for j in range(4):

        @pl.when(x <= (0, 1, 0, 2)[j])
        def _():
            take(pv.at[pl.ds(0, 7 * S), :], wx_send.at[j])

        for i in range(4):
            take(w_part(j, w_base(j, i), 2**i, core), wh_send.at[i, j])
        take(w_part(j, w_base(j, 3), 8, core), wd_send.at[j, 0])
        take(w_got(j, 3), wd_send.at[j, 1])
        for i in range(3):
            n = 2**i
            for g in range(2):
                take(a_part(j, addr[j] % 8 // n * n, n, g), ah_send.at[i, g, j])
        for g in range(4):
            take(fm.at[j * H : j * H + H, g * 2 * B : g * 2 * B + 2 * B], a3_send.at[g, j])
    take(pv.at[pl.ds(0, 15 * 2 * S), :], a1_send)
    take(pv.at[pl.ds(0, 7 * 4 * S), :], a2_send)
    for n in range(len(pieces)):
        xs, hf = pieces[n]
        take(pv, we_send.at[n])

        @pl.when(x == xs)
        def _():
            for d in range(3):
                take(pv, wr_send.at[n, d])

    for d in range(4):
        take(pv, ad_send.at[d])
        if d < 3:
            take(pv, ar_send.at[d])
    take(krow.at[:, 0 : 7 * H], kr_send)

    @pl.when(own)
    def _():
        take(ar.at[0:S, 0 : 15 * H], kc_send)

    local(wo, win_out, osem.at[0]).wait()
    local(po, pan_out, osem.at[1]).wait()
    for far in range(2):
        for k in range(4):
            half = addr[k] // 8
            if far:
                half = 1 - half
            at = pl.ds(pl.multiple_of(k * B + half * H, H), H)
            local(tr.at[:, at], trail_out.at[:, at], osem.at[2 + 4 * far + k]).wait()


def fused(live, win, inv, pan, trail):
    dma = pltpu.SemaphoreType.DMA
    anys = pl.BlockSpec(memory_space=pl.ANY)
    smem = pl.BlockSpec(memory_space=pltpu.SMEM)
    vmem = pltpu.VMEM
    return pl.pallas_call(
        kernel,
        out_shape=(
            jax.ShapeDtypeStruct((2 * B, B), BF),
            jax.ShapeDtypeStruct((N * B, B), BF),
            jax.ShapeDtypeStruct((2 * B, 4 * B), F32),
        ),
        in_specs=[smem] + [anys] * 4,
        out_specs=(anys,) * 3,
        scratch_shapes=[
            vmem((2 * B, B), BF),
            vmem((2 * B, B), BF),
            vmem((2 * B, B), BF),
            vmem((4 * S, N * B), BF),
            vmem((S, H), BF),
            vmem((S, N * H), BF),
            vmem((S, H), BF),
            vmem((2 * S, H), BF),
            vmem((B, B), BF),
            vmem((N * B, B), BF),
            vmem((N * B, N * B), BF),
            vmem((N * B, N * B), BF),
            vmem((N * B, N * B), BF),
            vmem((2 * B, N * B), BF),
            vmem((2 * B, N * B), BF),
            vmem((2 * B, N * B), BF),
            vmem((2 * B, N * B), BF),
            vmem((2 * B, N * B), BF),
            vmem((2 * B, 4 * B), F32),
            vmem((N * B, B), BF),
            vmem((2 * B, B), BF),
            dma((4,)), dma((4,)), dma((4, 4)), dma((4, 4)), dma((4, 2)), dma((4, 2)),
            dma((3,)), dma((3, 3)), dma((3,)), dma((3,)),
            dma(()), dma(()), dma((2,)), dma(()), dma((3, 2, 4)), dma((3, 2, 4)), dma((4, 4)), dma((4, 4)),
            dma((3,)), dma((3,)), dma((4,)), dma((4,)), dma(()), dma(()), dma((2,)), dma(()),
            dma((4,)), dma((10,)),
        ],
        compiler_params=pltpu.CompilerParams(
            has_side_effects=True, collective_id=0, vmem_limit_bytes=58 * 2**20
        ),
        name="fused",
    )(live, win, inv, pan, trail)


def hand_out_kernel(pan, win, trail, pan_out, win_out, trail_out, pv, wv, tv, load, store):
    parts = [(pan, pv, pan_out, 0, 512)]
    parts += [(win, wv, win_out, i * 1024, 1024) for i in range(2)]
    parts += [(trail, tv, trail_out, i * 64, 64) for i in range(8)]

    def move(n, inward):
        src, mid, dst, first, count = parts[n]
        at = slice(first, first + count)
        if inward:
            return pltpu.make_async_copy(src.at[at, :], mid.at[at, :], load.at[n])
        return pltpu.make_async_copy(mid.at[at, :], dst.at[at, :], store.at[n])

    for n in range(len(parts)):
        move(n, True).start()
    for n in range(len(parts)):
        move(n, True).wait()
        move(n, False).start()
    for n in range(len(parts)):
        move(n, False).wait()


def hand_out(*arrays):
    anys = pl.BlockSpec(memory_space=pl.ANY)
    dma = pltpu.SemaphoreType.DMA
    return pl.pallas_call(
        hand_out_kernel,
        out_shape=tuple(jax.ShapeDtypeStruct(a.shape, a.dtype) for a in arrays),
        in_specs=[anys] * 3,
        out_specs=(anys,) * 3,
        scratch_shapes=[pltpu.VMEM(a.shape, a.dtype) for a in arrays] + [dma((11,)), dma((11,))],
        name="hand_out",
    )(*arrays)


def local_part(panel_blocks, live_rows, window_blocks, diag_inverse, trailing):
    return hand_out(*fused(live_rows, window_blocks, diag_inverse[0], panel_blocks, trailing))


def solution(mesh):
    return jax.shard_map(
        local_part,
        mesh=mesh,
        in_specs=(
            P("row", "col"),
            P("col", "row"),
            P(None, "col"),
            P("col", None, None),
            P("row", "col"),
        ),
        out_specs=(P("row", "col"), P(None, "col"), P("row", "col")),
        check_vma=False,
    )
```

```python
import jax
import jax.numpy as jnp
from jax import lax
from jax.experimental import pallas as pl
from jax.experimental.pallas import tpu as pltpu
from jax.sharding import PartitionSpec as P

B = 256
S = 16
H = 128
N = 8
BF = jnp.bfloat16
F32 = jnp.float32
MESH = pl.DeviceIdType.MESH


def place():
    row = lax.axis_index("row")
    col = lax.axis_index("col")
    return row, col, col // 2, row % 4, row // 4, col % 2


def bits_of(y, z):
    return [((y + 1) // 2) % 2, ((z + 1) // 2) % 2, y // 2, z // 2]


def address(bits, k):
    return sum(bits[(k + i) % 4] * 2**i for i in range(4))


def partners(y, z):
    ya = y + 1 - 2 * (y % 2)
    za = z + 1 - 2 * (z % 2)
    return [z * 4 + ya, za * 4 + y, z * 4 + 3 - y, (3 - z) * 4 + y]


def pick(a, b, c):
    return a * (1 - c) + b * c


def lanes(c):
    return pl.ds(pl.multiple_of(c * B, B), B)


def rows(start, count):
    return pl.ds(pl.multiple_of(start, S), count)


def lane(p):
    return slice(p * B, p * B + B)


def nt(a, b):
    return lax.dot_general(a, b, (((1,), (1,)), ((), ())), preferred_element_type=F32)


def kernel(
    live, win, inv, pan, trail, pan_out, win_out, trail_out,
    pv, pp, st, a0, kp, krow, kf, kcol, iv, wc, wg, wf, u, ar, fr, am, fm, ao, tr, wo, po,
    wx_recv, wx_send, wh_recv, wh_send, wd_recv, wd_send, wr_recv, wr_send, we_recv, we_send,
    a1_recv, a1_send, a2_recv, a2_send, ah_recv, ah_send, a3_recv, a3_send,
    ar_recv, ar_send, ad_recv, ad_send, kr_recv, kr_send, kc_recv, kc_send, lsem, osem,
):
    row, col, x, y, z, core = place()
    bits = bits_of(y, z)
    addr = [address(bits, k) for k in range(4)]
    near = partners(y, z)
    other = 1 - core
    h = y % 2
    sibling = x * 2 + other
    own = (z == x) & (y // 2 == core)

    def local(src, dst, sem):
        return pltpu.make_async_copy(src, dst, sem)

    def take(ref, sem):
        pltpu.make_async_copy(ref, ref, sem).wait()

    def remote(src, dst, ssem, rsem, r, c):
        return pltpu.make_async_remote_copy(
            src_ref=src, dst_ref=dst, send_sem=ssem, recv_sem=rsem, device_id=(r, c), device_id_type=MESH
        )

    load = local(pan, pv, lsem.at[0])
    load.start()
    load_window = local(win, wc, lsem.at[1])
    load_window.start()
    load_inverse = local(inv, iv, lsem.at[3])
    load_inverse.start()
    load_trail = local(trail, tr, lsem.at[2])
    load_trail.start()

    barrier = pltpu.get_barrier_semaphore()

    def greet(r, c):
        pl.semaphore_signal(barrier, inc=1, device_id=(r, c), device_id_type=MESH)

    for d in range(1, 8):
        greet(row, (col + d) % 8)
    for d in range(1, 16):
        greet((row + d) % 16, col)

    l0 = live[0, 0]
    l1 = live[0, 1]
    load.wait()
    pv[B : 2 * B, :] = jnp.where(l0 == 1, pv[0:B, :], pv[B : 2 * B, :])
    keep0 = jnp.where(l0 == 0, 1.0, 0.0)
    keep1 = jnp.where((l0 == 1) | (l1 == 1), 1.0, 0.0)
    kp[...] = jnp.where(lax.broadcasted_iota(jnp.int32, (S, H), 0) == 0, keep0, keep1).astype(BF)
    for t in range(16):
        tbits = bits_of(t % 4, t // 4)
        for kk in range(2):
            s = pick(address(tbits, kk), address(tbits, 2 + kk), h)
            pp[t * 2 * S + kk * S : t * 2 * S + kk * S + S, :] = pv[rows(kk * B + s * S, S), :]

    pl.semaphore_wait(barrier, 22)

    mine = st.at[rows(row * 2 * S, 2 * S), :]
    local(pp.at[rows(row * 2 * S, 2 * S), :], mine, a1_recv).start()

    def scatter(d, carry):
        t = (row + d) % 16
        remote(pp.at[rows(t * 2 * S, 2 * S), :], mine, a1_send, a1_recv, t, col).start()
        return carry

    lax.fori_loop(1, 16, scatter, 0)

    kept = krow.at[:, pl.ds(pl.multiple_of(col * H, H), H)]
    local(kp, kept, kr_recv).start()
    for d in range(1, 8):
        remote(kp, kept, kr_send, kr_recv, row, (col + d) % 8).start()
    load_window.wait()
    load_inverse.wait()
    wc[lanes(col), :] = iv[...]
    for j in range(4):

        @pl.when(x <= (0, 1, 0, 2)[j])
        def _():
            for kc in range(2):
                t = addr[j] if kc == 0 else addr[3 - j]
                at = rows((2 * j + kc) * B + t * S, S)
                src = wc.at[at, :]
                dst = wg.at[at, lanes(col)]
                for d in range(4):
                    target = (x + d) % 4 * 2 + kc
                    if d == 0:

                        @pl.when(core == kc)
                        def _():
                            local(src, dst, wx_recv.at[j]).start()

                        @pl.when(core != kc)
                        def _():
                            remote(src, dst, wx_send.at[j], wx_recv.at[j], row, target).start()
                    else:
                        remote(src, dst, wx_send.at[j], wx_recv.at[j], row, target).start()

    def w_width(j):
        return (2, 4, 2, 6)[j] * B

    def w_base(j, i):
        n = 2**i
        return pick(addr[j], addr[3 - j], core) // n * n

    def w_part(j, base, n, c):
        return wg.at[rows((2 * j + c) * B + base * S, n * S), pl.ds(0, w_width(j))]

    def w_got(j, i):
        n = 2**i
        a = pick(addr[j], addr[3 - j], core)
        return w_part(j, a // (2 * n) * (2 * n) + (1 - a // n % 2) * n, n, core)

    def w_step(i):
        for j in range(4):
            if i == 0:
                take(w_part(j, w_base(j, 0), 1, core), wx_recv.at[j])
            else:
                take(w_got(j, i - 1), wh_recv.at[i - 1, j])
            part = w_part(j, w_base(j, i), 2**i, core)
            to = pick(near[(j + i) % 4], near[(3 - j + i) % 4], core)
            remote(part, part, wh_send.at[i, j], wh_recv.at[i, j], to, col).start()
            if i == 3:
                remote(part, part, wd_send.at[j, 0], wd_recv.at[j, 0], row, sibling).start()

    def a_part(k, base, n, g):
        return am.at[rows(k * H + base * S, n * S), slice(g * 4 * B, g * 4 * B + 4 * B)]

    def a_got(k, i, g):
        n = 2**i
        a = addr[k] % 8
        return a_part(k, a // (2 * n) * (2 * n) + (1 - a // n % 2) * n, n, g)

    def a_step(i, g):
        n = 2**i
        chunk = slice(g * 4 * B, g * 4 * B + 4 * B)
        if i == 0:
            take(a0.at[:, chunk], a2_recv.at[g])
            for k in range(4):
                am[rows(k * H + addr[k] % 8 * S, S), chunk] = a0[k * S : k * S + S, chunk]
        for k in range(4):
            if i > 0:
                take(a_got(k, i - 1, g), ah_recv.at[i - 1, g, k])
            if i < 3:
                part = a_part(k, addr[k] % 8 // n * n, n, g)
                remote(part, part, ah_send.at[i, g, k], ah_recv.at[i, g, k], near[(k + i) % 4], col).start()

    def a_last(g):
        for k in range(4):
            there = slice(k * H, k * H + H), slice(g * 2 * B, g * 2 * B + 2 * B)
            remote(fm.at[there], ao.at[there], a3_send.at[g, k], a3_recv.at[g, k], near[(k + 3) % 4], col).start()

    pieces = [(1, 0), (2, 0), (3, 1)]

    def piece(n, c):
        xs, hf = pieces[n]
        return (4 + 2 * hf) * B, lanes(2 * xs + c)

    def whole_send(n):
        xs, hf = pieces[n]

        @pl.when(x == xs)
        def _():
            first, at = piece(n, core)
            src = wc.at[first : first + 2 * B, :]
            dst = wg.at[first : first + 2 * B, at]
            local(src, dst, wr_recv.at[n]).start()
            for d in range(1, 4):
                remote(src, dst, wr_send.at[n, d - 1], wr_recv.at[n], row, (x + d) % 4 * 2 + core).start()

    def whole_share(n):
        xs, hf = pieces[n]
        first, at = piece(n, core)
        got = wg.at[first : first + 2 * B, at]
        take(got, wr_recv.at[n])
        remote(got, got, we_send.at[n], we_recv.at[n], row, sibling).start()

    def whole_take(n):
        first, at = piece(n, other)
        take(wg.at[first : first + 2 * B, at], we_recv.at[n])

    w_step(0)
    take(st, a1_recv)
    for d in range(4):
        xd = (x + d) % 4
        for kc in range(2):
            src = st.at[rows((4 * xd + 2 * kc) * 2 * S, 4 * S), :]
            dst = a0.at[:, lanes(col)]
            if d == 0:

                @pl.when(core == kc)
                def _():
                    local(src, dst, a2_recv.at[x // 2]).start()

                @pl.when(core != kc)
                def _():
                    remote(src, dst, a2_send, a2_recv.at[x // 2], row, sibling).start()
            else:
                remote(src, dst, a2_send, a2_recv.at[x // 2], row, xd * 2 + kc).start()

    w_step(1)
    take(krow, kr_recv)
    at_row = lax.broadcasted_iota(jnp.int32, (S, H), 0)
    flags = jnp.zeros((S, H), F32)
    for p in range(N):
        two = krow[:, p * H : p * H + H].astype(F32)
        for i in range(2):
            flags = jnp.where(at_row == 2 * p + i, two[i : i + 1, :], flags)
    kf[...] = flags.astype(BF)

    @pl.when(own)
    def _():
        dst = kcol.at[rows(h * S, S), :]
        local(kf, dst, kc_recv.at[h]).start()
        for d in range(1, 16):
            remote(kf, dst, kc_send, kc_recv.at[h], (row + d) % 16, col).start()

    a_step(0, 0)
    a_step(0, 1)
    for n in range(len(pieces)):
        whole_send(n)
    w_step(2)
    a_step(1, 0)
    a_step(1, 1)
    w_step(3)
    panel = ar.at[:, lanes(col)]
    local(pv, panel, lsem.at[0]).start()
    for d in range(1, 4):
        remote(pv, panel, ar_send.at[d - 1], ar_recv.at[d - 1], row, (x + d) % 4 * 2 + core).start()
    remote(pv, panel, ad_send.at[0], ad_recv.at[0], row, sibling).start()

    for j in range(4):
        got = w_got(j, 3)
        take(got, wh_recv.at[3, j])
        remote(got, got, wd_send.at[j, 1], wd_recv.at[j, 1], row, sibling).start()
    a_step(2, 0)
    a_step(2, 1)
    for n in range(len(pieces)):
        whole_share(n)
    for j in range(4):
        a = pick(addr[3 - j], addr[j], core) // 8
        take(w_part(j, a * 8, 8, other), wd_recv.at[j, 0])
        take(w_part(j, (1 - a) * 8, 8, other), wd_recv.at[j, 1])

    def keep(ref, first, i, p):
        t = ref[first : first + S, :].astype(F32)[2 * p + i : 2 * p + i + 1, :]
        return jnp.concatenate([t, t], axis=1) > 0.5

    def masked(value, mask):
        return jnp.where(mask, value, 0.0).astype(BF)

    def operand(factors, raw, at, p):
        if p == 0:
            return raw[at, lane(p)]
        return jnp.concatenate([factors[at, : p * B], raw[at, lane(p)]], axis=1)

    take(kcol.at[0:S, :], kc_recv.at[0])
    take(kcol.at[S : 2 * S, :], kc_recv.at[1])

    def solve(p, factors, raw):
        up = u[lane(p), : (p + 1) * B]
        out = nt(operand(factors, raw, slice(0, 2 * B), p), up)
        for k in range(4):
            part = slice(k * H, k * H + H)
            factors[part, lane(p)] = masked(out[part, :], keep(kcol, k // 2 * S, k % 2, p))

    for p in range(N):
        if p == 2:
            whole_take(0)
        if p == 4:
            whole_take(1)
        if p == 6:
            whole_take(2)
        diag = wg[lane(p), lane(p)]
        if p > 0:
            prev = jnp.dot(diag, wf[lane(p), : p * B], preferred_element_type=F32)
            u[lane(p), : p * B] = (-prev).astype(BF)
        u[lane(p), lane(p)] = diag
        up = u[lane(p), : (p + 1) * B]
        for q in range(p + 1, N):
            wf[lane(q), lane(p)] = nt(operand(wf, wg, lane(q), p), up).astype(BF)
        if p == 4:
            a_step(3, 0)
        if p == 6:
            a_step(3, 1)
        for p2 in ((), (), (), (), (0, 1), (2, 3), (4, 5), (6, 7))[p]:
            solve(p2, fm, am)
            if p2 % 2 == 1:
                a_last(p2 // 2)

    here = lanes(col)
    for q in range(N):
        block = wf[lane(q), here]
        wo[lane(q), :] = jnp.where(q > col, block, jnp.zeros_like(block))
    local(wo, win_out, osem.at[0]).start()

    def update(factors, far, first, last):
        for g in range(2):
            prod = nt(fr[:, first:last], factors[lane(g), first:last])
            for e in range(2):
                k = 2 * g + e
                half = addr[k] // 8
                if far:
                    half = 1 - half
                at = pl.ds(pl.multiple_of(k * B + half * H, H), H)
                tr[:, at] = tr[:, at] - prod[:, e * H : e * H + H]
                if last == N * B:
                    local(tr.at[:, at], trail_out.at[:, at], osem.at[2 + 4 * far + k]).start()

    def take_far(g):
        for k in range(4):
            take(ao.at[k * H : k * H + H, g * 2 * B : g * 2 * B + 2 * B], a3_recv.at[g, k])

    for d in range(1, 4):
        got = ar.at[:, lanes((x + 4 - d) % 4 * 2 + core)]
        take(got, ar_recv.at[d - 1])
        remote(got, got, ad_send.at[d], ad_recv.at[d], row, sibling).start()
    local(pv, panel, lsem.at[0]).wait()
    for d in range(4):
        take(ar.at[:, lanes((x + 4 - d) % 4 * 2 + other)], ad_recv.at[d])
    for p in range(N):
        up = u[lane(p), : (p + 1) * B]
        for i in range(2):
            fr[lane(i), lane(p)] = masked(nt(operand(fr, ar, lane(i), p), up), keep(kf, 0, i, p))
    f0 = fr[0:B, here]
    f1 = fr[B : 2 * B, here]
    po[0:B, :] = jnp.where(l0 == 0, f0, f1)
    po[B : 2 * B, :] = jnp.where(l0 == 0, f1, jnp.zeros_like(f1))
    local(po, pan_out, osem.at[1]).start()

    load_trail.wait()
    update(fm, 0, 0, N * B)

    for g in range(3):
        take_far(g)
    update(ao, 1, 0, 6 * B)
    take_far(3)
    update(ao, 1, 6 * B, N * B)

    for j in range(4):

        @pl.when(x <= (0, 1, 0, 2)[j])
        def _():
            take(pv.at[pl.ds(0, 7 * S), :], wx_send.at[j])

        for i in range(4):
            take(w_part(j, w_base(j, i), 2**i, core), wh_send.at[i, j])
        take(w_part(j, w_base(j, 3), 8, core), wd_send.at[j, 0])
        take(w_got(j, 3), wd_send.at[j, 1])
        for i in range(3):
            n = 2**i
            for g in range(2):
                take(a_part(j, addr[j] % 8 // n * n, n, g), ah_send.at[i, g, j])
        for g in range(4):
            take(fm.at[j * H : j * H + H, g * 2 * B : g * 2 * B + 2 * B], a3_send.at[g, j])
    take(pv.at[pl.ds(0, 15 * 2 * S), :], a1_send)
    take(pv.at[pl.ds(0, 7 * 4 * S), :], a2_send)
    for n in range(len(pieces)):
        xs, hf = pieces[n]
        take(pv, we_send.at[n])

        @pl.when(x == xs)
        def _():
            for d in range(3):
                take(pv, wr_send.at[n, d])

    for d in range(4):
        take(pv, ad_send.at[d])
        if d < 3:
            take(pv, ar_send.at[d])
    take(krow.at[:, 0 : 7 * H], kr_send)

    @pl.when(own)
    def _():
        take(ar.at[0:S, 0 : 15 * H], kc_send)

    local(wo, win_out, osem.at[0]).wait()
    local(po, pan_out, osem.at[1]).wait()
    for far in range(2):
        for k in range(4):
            half = addr[k] // 8
            if far:
                half = 1 - half
            at = pl.ds(pl.multiple_of(k * B + half * H, H), H)
            local(tr.at[:, at], trail_out.at[:, at], osem.at[2 + 4 * far + k]).wait()


def fused(live, win, inv, pan, trail):
    dma = pltpu.SemaphoreType.DMA
    anys = pl.BlockSpec(memory_space=pl.ANY)
    smem = pl.BlockSpec(memory_space=pltpu.SMEM)
    vmem = pltpu.VMEM
    return pl.pallas_call(
        kernel,
        out_shape=(
            jax.ShapeDtypeStruct((2 * B, B), BF),
            jax.ShapeDtypeStruct((N * B, B), BF),
            jax.ShapeDtypeStruct((2 * B, 4 * B), F32),
        ),
        in_specs=[smem] + [anys] * 4,
        out_specs=(anys,) * 3,
        scratch_shapes=[
            vmem((2 * B, B), BF),
            vmem((2 * B, B), BF),
            vmem((2 * B, B), BF),
            vmem((4 * S, N * B), BF),
            vmem((S, H), BF),
            vmem((S, N * H), BF),
            vmem((S, H), BF),
            vmem((2 * S, H), BF),
            vmem((B, B), BF),
            vmem((N * B, B), BF),
            vmem((N * B, N * B), BF),
            vmem((N * B, N * B), BF),
            vmem((N * B, N * B), BF),
            vmem((2 * B, N * B), BF),
            vmem((2 * B, N * B), BF),
            vmem((2 * B, N * B), BF),
            vmem((2 * B, N * B), BF),
            vmem((2 * B, N * B), BF),
            vmem((2 * B, 4 * B), F32),
            vmem((N * B, B), BF),
            vmem((2 * B, B), BF),
            dma((4,)), dma((4,)), dma((4, 4)), dma((4, 4)), dma((4, 2)), dma((4, 2)),
            dma((3,)), dma((3, 3)), dma((3,)), dma((3,)),
            dma(()), dma(()), dma((2,)), dma(()), dma((3, 2, 4)), dma((3, 2, 4)), dma((4, 4)), dma((4, 4)),
            dma((3,)), dma((3,)), dma((4,)), dma((4,)), dma(()), dma(()), dma((2,)), dma(()),
            dma((4,)), dma((10,)),
        ],
        compiler_params=pltpu.CompilerParams(
            has_side_effects=True, collective_id=0, vmem_limit_bytes=58 * 2**20
        ),
        name="fused",
    )(live, win, inv, pan, trail)


def hand_out_kernel(pan, win, trail, pan_out, win_out, trail_out, pv, wv, tv, load, store):
    parts = [(pan, pv, pan_out, 0, 512)]
    parts += [(win, wv, win_out, i * 1024, 1024) for i in range(2)]
    parts += [(trail, tv, trail_out, i * 64, 64) for i in range(8)]

    def move(n, inward):
        src, mid, dst, first, count = parts[n]
        at = slice(first, first + count)
        if inward:
            return pltpu.make_async_copy(src.at[at, :], mid.at[at, :], load.at[n])
        return pltpu.make_async_copy(mid.at[at, :], dst.at[at, :], store.at[n])

    for n in range(len(parts)):
        move(n, True).start()
    for n in range(len(parts)):
        move(n, True).wait()
        move(n, False).start()
    for n in range(len(parts)):
        move(n, False).wait()


def hand_out(*arrays):
    anys = pl.BlockSpec(memory_space=pl.ANY)
    dma = pltpu.SemaphoreType.DMA
    return pl.pallas_call(
        hand_out_kernel,
        out_shape=tuple(jax.ShapeDtypeStruct(a.shape, a.dtype) for a in arrays),
        in_specs=[anys] * 3,
        out_specs=(anys,) * 3,
        scratch_shapes=[pltpu.VMEM(a.shape, a.dtype) for a in arrays] + [dma((11,)), dma((11,))],
        name="hand_out",
    )(*arrays)


def local_part(panel_blocks, live_rows, window_blocks, diag_inverse, trailing):
    return hand_out(*fused(live_rows, window_blocks, diag_inverse[0], panel_blocks, trailing))


def solution(mesh):
    return jax.shard_map(
        local_part,
        mesh=mesh,
        in_specs=(
            P("row", "col"),
            P("col", "row"),
            P(None, "col"),
            P("col", None, None),
            P("row", "col"),
        ),
        out_specs=(P("row", "col"), P(None, "col"), P("row", "col")),
        check_vma=False,
    )
```
